128 devices in a mesh: ha: 128 (over y, x, z, core).
Axes of the slice: x: 4, y: 4, z: 4, core: 2. Of those that a mesh axis runs over, the one named last changes fastest.
Arguments:
- density: float32 [4096, 18432], P('ha'), may hold values from -6 to 6
- up_link: int32 [4096, 40], P('ha'), may hold values from -1 to 4095, as said below
- down_link: int32 [4096, 40], P('ha'), may hold values from -1 to 4095, as said below
- occupation: int32 [4096, 40], P('ha'), may hold values from 0 to 3, as said below
- pigments: int32 [40], replicated, may hold values from 0 to 95
- hamiltonian: float32 [96, 96], replicated, as said below
- dipole: float32 [96, 96], replicated, as said below
- damping_rates: float32 [40], replicated, may hold values from 0.05 to 0.5
- coupling_re: float32 [40], replicated, may hold values from 0.3 to 1.5
- coupling_im: float32 [40], replicated, may hold values from -1 to 1
- field: float32 [64], replicated, may hold values from -1.5 to 1.5
- pulse_steps: int32 [2], replicated, may hold values from 0 to 63
Outputs:
- evolved: float32 [4096, 18432], P('ha')
The draws below stay inside these ranges and needn't reach their ends.
Inputs may be any that keep to these rules, and one draw needn't show every extreme that they name: The auxiliaries are the occupation vectors over the 40 modes whose occupations sum to at most 3: in a fixed order of the modes, the first 4096 of them taken by total occupation and then lexicographically. The p-th of them lies on device sigma(p mod 128), at a slot of that device, with sigma a permutation of the devices; the slots and the labels of the modes are permuted as well. up_link[a, k] is the auxiliary with occupation of mode k raised by one if that one is among them, else -1 (always -1 where the total is 3). `down_link`: the auxiliary with occupation of mode k lowered by one, -1 where that occupation is 0; the inverse of up_link. `occupation`: each row sums to at most 3. `hamiltonian`: Symmetric, diagonal energies of order one and off-diagonal couplings. `dipole`: Symmetric.
All inputs are finite; a program needn't handle non-finite values.
Results may differ from the reference program's by a relative error of at most 0.0003.
Values sent between devices are 32-bit elements; how exact they have to be, the bound alone decides.
No kernel may reach another device: no remote copies, remote signals or barrier semaphores. Data moves between devices by JAX's collectives and lax.ppermute only.
A program may use at most 128 MiB of HBM per device.

```python
import math
import jax
import jax.numpy as jnp
import numpy as np
from jax import lax

M = 96
K = 40
DEPTH = 3
NT = 64
AUX_DEV = 32
AUX = 4096
N_HA = 128


def canon_links(modes, depth, count):
    sentinel = modes
    tiers = [np.full((1, depth), sentinel, np.int64)]
    for level in range(1, depth + 1):
        previous = tiers[-1]
        if level > 1:
            latest = previous[:, level - 2]
        else:
            latest = np.zeros(previous.shape[0], np.int64)
        extra = np.tile(np.arange(modes, dtype=np.int64), previous.shape[0])
        repeated = np.repeat(previous, modes, axis=0)
        keep = extra >= np.repeat(latest, modes)
        grown = repeated[keep].copy()
        grown[:, level - 1] = extra[keep]
        tiers.append(grown)
    members = np.concatenate(tiers, axis=0)[:count]
    radix = modes + 1
    powers = radix ** np.arange(depth, dtype=np.int64)
    lookup = np.full(radix ** depth, -1, np.int64)
    lookup[np.sum(members * powers, axis=1)] = np.arange(count, dtype=np.int64)
    filled = np.sum(members < sentinel, axis=1)
    rows_all = np.arange(count)
    up_table = np.full((count, modes), -1, np.int64)
    down_table = np.full((count, modes), -1, np.int64)
    occupied = np.zeros((count, modes), np.int64)
    for mode in range(modes):
        holds = np.sum(members == mode, axis=1)
        occupied[:, mode] = holds
        added = members.copy()
        added[rows_all, np.minimum(filled, depth - 1)] = mode
        added = np.sort(added, axis=1)
        up_table[:, mode] = np.where(filled < depth, lookup[np.sum(added * powers, axis=1)], -1)
        removed = members.copy()
        removed[rows_all, np.argmax(members == mode, axis=1)] = sentinel
        removed = np.sort(removed, axis=1)
        down_table[:, mode] = np.where(holds > 0, lookup[np.sum(removed * powers, axis=1)], -1)
    return (up_table, down_table, occupied)


def build_links(key):
    count = AUX_DEV * N_HA
    up_c, down_c, occ_c = canon_links(K, DEPTH, count)
    key_mode = jax.random.fold_in(key, 101)
    key_dev = jax.random.fold_in(key, 102)
    key_slot = jax.random.fold_in(key, 103)
    relabel = jax.random.permutation(key_mode, K).astype(jnp.int32)
    columns = jnp.argsort(relabel, stable=True).astype(jnp.int32)
    dev_perm = jax.random.permutation(key_dev, N_HA).astype(jnp.int32)
    slot_perm = jax.vmap(lambda sub: jax.random.permutation(sub, AUX_DEV))(jax.random.split(key_slot, N_HA)).astype(jnp.int32)
    position = jnp.arange(count, dtype=jnp.int32)
    home = dev_perm[position % N_HA]
    where_to = home * AUX_DEV + slot_perm[home, position // N_HA]

    def place(table, linked):
        table = jnp.asarray(table, jnp.int32)
        if linked:
            table = jnp.where(table >= 0, where_to[jnp.maximum(table, 0)], -1).astype(jnp.int32)
        table = table[:, columns]
        return jnp.zeros((count, K), jnp.int32).at[where_to].set(table)
    return (place(up_c, True), place(down_c, True), place(occ_c, False))


def draw_up_link(key, part):
    up, down, level = build_links(key)
    return up


def draw_down_link(key, part):
    up, down, level = build_links(key)
    return down


def draw_occupation(key, part):
    up, down, level = build_links(key)
    return level


def symmetric(key, diag_scale, off_scale):
    key_diag, key_off = jax.random.split(key)
    off = jax.random.normal(key_off, (M, M), jnp.float32) * (off_scale * M ** (-0.5))
    off = 0.5 * (off + off.T)
    diag = jax.random.uniform(key_diag, (M,), jnp.float32, -diag_scale, diag_scale)
    return off + jnp.diag(diag)


def draw_hamiltonian(key, part):
    key = jax.random.fold_in(key, 11)
    return symmetric(key, 1.0, 1.0)


def draw_dipole(key, part):
    key = jax.random.fold_in(key, 12)
    return symmetric(key, 0.8, 1.2)


def set_ends(values, key, low, high):
    spot = [jax.random.randint(jax.random.fold_in(key, axis), (), 0, length) for axis, length in enumerate(values.shape)]
    longest = values.shape.index(max(values.shape))
    next_to = spot[:longest] + [(spot[longest] + 1) % values.shape[longest]] + spot[longest + 1:]
    return values.at[tuple(spot)].set(low).at[tuple(next_to)].set(high)


def block_scale(own_key, extent, cuts, smallest, largest):
    loudness, own = 1.0, jax.random.fold_in(own_key, 6)
    for dim, blocks in cuts:
        heights = jnp.exp(jax.random.uniform(jax.random.fold_in(own, dim), (blocks,), jnp.float32, smallest / len(cuts), largest / len(cuts)))
        loudness = loudness * jnp.repeat(heights, extent[dim] // blocks).reshape([-1 if axis == dim else 1 for axis in range(len(extent))])
    return loudness


def bell_draw(rng, extent, scale, most, cuts=(), kind=jnp.bfloat16):
    entries = jax.random.normal(rng, extent, jnp.float32) * scale
    if len(cuts) > 0:
        entries = block_scale(rng, extent, cuts, -0.22, 0.18) * entries
    return jnp.clip(entries, min=-most, max=most).astype(kind)


def setup_inputs(seed: int = 0) -> dict:
    streams_of = jax.random.split(jax.random.key(seed), 13)
    density = bell_draw(streams_of[0], (AUX, 2 * M * M), 1.0, 6.0, ((0, 128),), jnp.float32)
    up_link = draw_up_link(jax.random.fold_in(streams_of[12], 71), 0)
    down_link = draw_down_link(jax.random.fold_in(streams_of[12], 71), 0)
    occupation = draw_occupation(jax.random.fold_in(streams_of[12], 71), 0)
    pigments = set_ends(jax.random.randint(streams_of[4], (K,), 0, M), jax.random.fold_in(streams_of[4], 1), 0, M - 1).astype(jnp.int32)
    hamiltonian = draw_hamiltonian(jax.random.fold_in(streams_of[12], 71), 0)
    dipole = draw_dipole(jax.random.fold_in(streams_of[12], 71), 0)
    damping_rates = jnp.clip(jnp.exp(jax.random.uniform(streams_of[7], (K,), jnp.float32, math.log(0.05), math.log(0.5))), 0.05, 0.5)
    coupling_re = jnp.clip(jnp.exp(jax.random.uniform(streams_of[8], (K,), jnp.float32, math.log(0.3), math.log(1.5))), 0.3, 1.5)
    coupling_im = jnp.clip(jax.random.uniform(streams_of[9], (K,), jnp.float32, -1.0, 1.0), -1.0, 1.0)
    field = jnp.clip(jax.random.uniform(streams_of[10], (NT,), jnp.float32, -1.5, 1.5), -1.5, 1.5)
    pulse_steps = jax.random.randint(streams_of[11], (2,), 0, NT).astype(jnp.int32)
    return {"density": density, "up_link": up_link, "down_link": down_link, "occupation": occupation, "pigments": pigments, "hamiltonian": hamiltonian, "dipole": dipole, "damping_rates": damping_rates, "coupling_re": coupling_re, "coupling_im": coupling_im, "field": field, "pulse_steps": pulse_steps}


step_length = 0.1


def serve(state, codes, width):
    valid = codes > 0
    flat = jnp.maximum(codes - 1, 0)
    slot = flat // width
    pig = flat % width
    rows = state[slot, pig, :]
    col_re = state[slot, :, pig]
    col_im = state[slot, :, pig + width]
    message = jnp.concatenate([rows, col_re, col_im], axis=-1)
    return jnp.where(valid[..., None], message, jnp.float32(0.0))


def derivative(state, hmat, up_msg, down_msg, level, rates, coup_re, coup_im, onehot, width):
    count = state.shape[0]
    high = lax.Precision.HIGHEST
    left = jnp.einsum('ij,ajk->aik', hmat, state, precision=high)
    right = jnp.einsum('aipj,jk->aipk', state.reshape(count, width, 2, width), hmat, precision=high).reshape(count, width, 2 * width)
    d_re = left[..., width:] - right[..., width:]
    d_im = right[..., :width] - left[..., :width]
    lvl = level.astype(jnp.float32)
    decay = jnp.sum(lvl * rates[None, :], axis=1)[:, None, None]
    ur_re = up_msg[..., :width]
    ur_im = up_msg[..., width:2 * width]
    uc_re = up_msg[..., 2 * width:3 * width]
    uc_im = up_msg[..., 3 * width:]
    pr_re = down_msg[..., :width]
    pr_im = down_msg[..., width:2 * width]
    pc_re = down_msg[..., 2 * width:3 * width]
    pc_im = down_msg[..., 3 * width:]
    scale_a = (lvl * coup_re[None, :])[..., None]
    scale_b = (lvl * coup_im[None, :])[..., None]
    row_re = ur_im + scale_a * pr_im + scale_b * pr_re
    col_re = -uc_im - scale_a * pc_im + scale_b * pc_re
    row_im = -ur_re - scale_a * pr_re + scale_b * pr_im
    col_im = uc_re + scale_a * pc_re + scale_b * pc_im
    d_re = d_re + jnp.einsum('km,akj->amj', onehot, row_re, precision=high) + jnp.einsum('aki,km->aim', col_re, onehot, precision=high)
    d_im = d_im + jnp.einsum('km,akj->amj', onehot, row_im, precision=high) + jnp.einsum('aki,km->aim', col_im, onehot, precision=high)
    return jnp.concatenate([d_re, d_im], axis=-1) - decay * state


def reference(density, up_link, down_link, occupation, pigments, hamiltonian, dipole, damping_rates, coupling_re, coupling_im, field, pulse_steps):
    width = hamiltonian.shape[0]
    modes = pigments.shape[0]
    flat_shape = density.shape
    start = density.reshape(flat_shape[0], width, 2 * width)
    up_codes = jnp.where(up_link >= 0, up_link * width + pigments[None, :] + 1, 0).astype(jnp.int32)
    down_codes = jnp.where(down_link >= 0, down_link * width + pigments[None, :] + 1, 0).astype(jnp.int32)
    onehot = (pigments[:, None] == jnp.arange(width, dtype=jnp.int32)[None, :]).astype(jnp.float32)

    def rate(state, hmat):
        def block(pieces):
            span_state, span_up, span_down, span_level = pieces
            return derivative(span_state, hmat, serve(state, span_up, width), serve(state, span_down, width), span_level, damping_rates, coupling_re, coupling_im, onehot, width)

        blocks = lax.map(block, (state.reshape(N_HA, AUX_DEV, width, 2 * width), up_codes.reshape(N_HA, AUX_DEV, modes), down_codes.reshape(N_HA, AUX_DEV, modes), occupation.reshape(N_HA, AUX_DEV, modes)))
        return blocks.reshape(state.shape)

    first_h = hamiltonian + field[pulse_steps[0]] * dipole
    second_h = hamiltonian + field[pulse_steps[1]] * dipole
    first = rate(start, first_h)
    middle = start + (0.5 * step_length) * first
    second = rate(middle, second_h)
    return (start + step_length * second).reshape(flat_shape)
```

```python
import functools

import jax
import jax.numpy as jnp
from jax import lax
from jax.experimental import pallas as pl
from jax.experimental.pallas import tpu as pltpu
from jax.sharding import PartitionSpec as P

M = 96
K = 40
A = 32
N = 128
Q = K * A
LIST = 192
C = 15
WIDE = 512
PIECES = 3 * C + 1
TAG = 96
HALF = 0.05
STEP = 0.1

f32, bf16, i32 = jnp.float32, jnp.bfloat16, jnp.int32
VMEM = pl.BlockSpec(memory_space=pltpu.VMEM)
SMEM = pl.BlockSpec(memory_space=pltpu.SMEM)


def iota(shape, axis):
    return lax.broadcasted_iota(i32, shape, axis)


def dot(a, b):
    return jnp.dot(a, b, preferred_element_type=f32)


def split(x):
    high = x.astype(bf16)
    return high, (x - high.astype(f32)).astype(bf16)


def pick(ones, x):
    high, low = split(x)
    return dot(ones, high) + dot(ones, low)


def spread(x, ones):
    high, low = split(x)
    return dot(high, ones) + dot(low, ones)


def onehot(mask):
    return jnp.where(mask, 1.0, 0.0).astype(bf16)


def widen(o0, o1, o2):
    lane = iota(o0.shape, 1)
    keep = lane < M
    t1 = pltpu.roll(jnp.where(lane >= 96, o0, o1), 32, 1)
    t2 = pltpu.roll(jnp.where(lane >= 64, o1, o2), 64, 1)
    t3 = pltpu.roll(o2, 96, 1)
    return [jnp.where(keep, t, 0.0) for t in (o0, t1, t2, t3)]


def narrow(t0, t1, t2, t3):
    lane = iota(t0.shape, 1)
    r1, r2, r3 = pltpu.roll(t1, 96, 1), pltpu.roll(t2, 64, 1), pltpu.roll(t3, 32, 1)
    return jnp.where(lane < 96, t0, r1), jnp.where(lane < 64, r1, r2), jnp.where(lane < 32, r2, r3)


def tile(x, j):
    return x[:, j * 128 : (j + 1) * 128]


def both(ref):
    return jnp.concatenate([ref[0], ref[1]], axis=1)


def pigment_columns(pig):
    lane = iota((1, 128), 1)
    at = jnp.full((1, 128), -1, i32)
    for k in range(K):
        at = jnp.where(lane == k, pig[k], at)
        at = jnp.where(lane == K + k, pig[k] + 128, at)
    return jnp.where(iota((256, 128), 0) == at, 1.0, 0.0)


def plan(links, coef, listed, slots):
    before = onehot(iota((256, 256), 0) < iota((256, 256), 1))
    device = iota((N, 256), 0)
    carry = jnp.zeros((N, 1), f32)
    order = iota((LIST, 256), 0)
    total = [jnp.zeros((LIST, 256), f32) for _ in range(4)]
    for h in range(2):
        for t in range(Q // 256):
            span = pl.ds(t * 256, 256)
            link = links[h : h + 1, span]
            dest = lax.shift_right_arithmetic(link, 5)
            mine = dest == device
            ones = jnp.where(mine, 1.0, 0.0)
            count = dot(ones.astype(bf16), before) + carry
            carry = count[:, 255:256] + ones[:, 255:256]
            rank = jnp.sum(jnp.where(mine, count, 0.0), axis=0, keepdims=True)
            place = jnp.sum(count, axis=0, keepdims=True).astype(i32)
            place = jnp.where(link >= 0, place, -1)
            slot = rank * N + dest.astype(f32)
            mode = lax.shift_right_arithmetic(iota((1, 256), 1) + t * 256, 5)
            tag = (mode * A + (link & 31) + 1).astype(f32)
            here = order == place
            new = jnp.where(here, 1.0, 0.0)
            listed[:, span] = new if h == 0 else listed[:, span] + new
            total[0] += jnp.where(here, slot, 0.0)
            total[1] += jnp.where(here, tag, 0.0)
            if h == 0:
                total[2] += jnp.where(here, coef[0:1, span], 0.0)
                total[3] += jnp.where(here, coef[1:2, span], 0.0)
            else:
                total[2] += new
    lane = iota((LIST, 128), 1)
    out = jnp.zeros((LIST, 128), f32)
    for j in range(4):
        out = jnp.where(lane == j, jnp.sum(total[j], axis=1, keepdims=True), out)
    slots[...] = jnp.where((lane == 0) & (out[:, 1:2] == 0.0), -1.0, out)


def pack(state, pig, columns, listed, slots, table, work, send):
    work[...] = spread(both(state), columns.astype(bf16))
    for k in range(K):
        for h in range(2):
            rows = pl.ds(pl.multiple_of(pig[k] * A, A), A)
            table[h, pl.ds(k * A, A), :] = state[h, rows, :]
    blank = jnp.zeros((128 - M, 128), f32)
    for a in range(A):
        block = jnp.concatenate([work[pl.ds(a, M, stride=A), :], blank], axis=0).T
        table[2, pl.ds(a, K, stride=A), :] = block[0:K]
        table[3, pl.ds(a, K, stride=A), :] = block[K : 2 * K]
    message = pick(listed[...].astype(bf16), jnp.concatenate([table[j] for j in range(4)], axis=1))
    info = slots[...]
    sa, sb = info[:, 2:3], info[:, 3:4]
    x0, x1, x2, x3 = (tile(message, j) for j in range(4))
    x0, x1, x2, x3 = sa * x1 + sb * x0, sb * x1 - sa * x0, sb * x2 - sa * x3, sa * x2 + sb * x3
    x0 = jnp.where(iota((LIST, 128), 1) == TAG, info[:, 1:2], x0)
    message = jnp.concatenate([x0, x1, x2, x3], axis=1)
    high, low = split(message)
    goal = info.T[0:1, :].astype(i32)
    lane = iota((N, 128), 1)
    tags = jnp.zeros((N, 128), f32)
    for r in range(C):
        ones = onehot(iota((N, LIST), 0) + r * N == goal)
        part = dot(ones, high) + dot(ones, low)
        tags = jnp.where(lane == r, pltpu.roll(tile(part, 0), (r - TAG) % 128, 1), tags)
        for j, piece in enumerate(narrow(*(tile(part, j) for j in range(4)))):
            send[pl.ds(3 * r + j, N, stride=PIECES), :] = piece
    send[pl.ds(3 * C, N, stride=PIECES), :] = tags


def receive(got):
    tags = got[pl.ds(3 * C, N, stride=PIECES), :]
    across = tags.T
    before = onehot(iota((128, 128), 0) < iota((128, 128), 1))
    lane = iota((N, 128), 1)
    carry = jnp.zeros((1, 1), f32)
    order = iota((LIST, 128), 0)
    out = jnp.zeros((LIST, WIDE), f32)
    full = onehot(across[0:16, :] > 0.5)
    count = dot(full, before)
    for r in range(C):
        tag = across[r : r + 1, :]
        ones = jnp.where(tag > 0.5, 1.0, 0.0)
        place = jnp.where(tag > 0.5, (count[r : r + 1, :] + carry).astype(i32), -1)
        carry = carry + count[r : r + 1, 127:128] + ones[:, 127:128]
        t0, t1, t2, t3 = widen(*(got[pl.ds(3 * r + j, N, stride=PIECES), :] for j in range(3)))
        t0 = jnp.where(lane == TAG, pltpu.roll(tags, TAG - r, 1), t0)
        out = out + pick(onehot(order == place), jnp.concatenate([t0, t1, t2, t3], axis=1))
    return out


def put(message, pig, columns, dense, work, total):
    tag = message[:, 0:128].T[TAG : TAG + 1, :].astype(i32)
    clean = jnp.where((iota(message.shape, 1) & 127) < M, message, 0.0)
    placed = pick(onehot(iota((Q, message.shape[0]), 0) + 1 == tag), clean)
    for j in range(4):
        dense[j] = tile(placed, j)
    blank = jnp.zeros((128 - 2 * K, 128), f32)
    for a in range(A):
        rows = pl.ds(a, K, stride=A)
        block = jnp.concatenate([dense[2, rows, :], dense[3, rows, :], blank], axis=0).T
        work[pl.ds(a, M, stride=A), :] = block[0:M]
    added = spread(work[...], columns.T.astype(bf16))
    for h in range(2):
        total[h] += tile(added, h)
    for k in range(K):
        for h in range(2):
            rows = pl.ds(pl.multiple_of(pig[k] * A, A), A)
            total[h, rows, :] += dense[h, pl.ds(k * A, A), :]


def open_kernel(pig, links, coef, density, state, send, listed, slots, table, work):
    plan(links, coef, listed, slots)
    for m in range(M // 2):
        parts = widen(*(density[:, m * 384 + j * 128 : m * 384 + (j + 1) * 128] for j in range(3)))
        for j in range(2):
            for h in range(2):
                state[h, pl.ds((2 * m + j) * A, A), :] = parts[2 * j + h]
    pack(state, pig, pigment_columns(pig), listed, slots, table, work, send)


def commutator_kernel(section, field, steps, decay, hamiltonian, dipole, state, out, twice):
    h = hamiltonian[...] + field[steps[section]] * dipole[...]
    twice[...] = jnp.zeros((256, 256), f32)
    twice[0:M, 0:M] = h
    twice[128 : 128 + M, 128 : 128 + M] = h
    hh, hl = split(h)
    bh, bl = split(twice[...])

    def body(a, _):
        rows = pl.ds(a, M, stride=A)
        x = jnp.concatenate([state[0, rows, :], state[1, rows, :]], axis=1)
        xh, xl = split(x)
        left = dot(hh, xh) + dot(hl, xh) + dot(hh, xl)
        right = dot(xh, bh) + dot(xh, bl) + dot(xl, bh)
        d = left - right
        rate = decay[a]
        out[0, rows, :] = d[:, 128:256] - rate * x[:, 0:128]
        out[1, rows, :] = -d[:, 0:128] - rate * x[:, 128:256]
        return _

    lax.fori_loop(0, A, body, 0, unroll=4)


def middle_kernel(pig, got, state, rate, listed, slots, middle, send, dense, work):
    columns = pigment_columns(pig)
    message = receive(got)
    middle[...] = rate[...]
    put(message, pig, columns, dense, work, middle)
    middle[...] = state[...] + HALF * middle[...]
    pack(middle, pig, columns, listed, slots, dense, work, send)


def close_kernel(pig, got, state, rate, out, total, dense, work):
    message = receive(got)
    total[...] = rate[...]
    put(message, pig, pigment_columns(pig), dense, work, total)
    for m in range(M // 2):
        parts = []
        for j in range(2):
            rows = pl.ds((2 * m + j) * A, A)
            for half in range(2):
                parts.append(state[half, rows, :] + STEP * total[half, rows, :])
        for j, piece in enumerate(narrow(*parts)):
            out[:, m * 384 + j * 128 : m * 384 + (j + 1) * 128] = piece


def call(kernel, in_specs, outs, scratch):
    return pl.pallas_call(
        kernel,
        in_specs=in_specs,
        out_specs=[VMEM] * len(outs),
        out_shape=[jax.ShapeDtypeStruct(*o) for o in outs],
        scratch_shapes=[pltpu.VMEM(*s) for s in scratch],
        compiler_params=pltpu.CompilerParams(vmem_limit_bytes=48 * 1024 * 1024),
    )


def exchange(send):
    got = lax.all_to_all(
        send.reshape(N, 1, PIECES * 128), "ha", split_axis=0, concat_axis=0, tiled=True
    )
    return got.reshape(N * PIECES, 128)


def on_device(
    density,
    up_link,
    down_link,
    occupation,
    pigments,
    hamiltonian,
    dipole,
    damping_rates,
    coupling_re,
    coupling_im,
    field,
    pulse_steps,
):
    links = jnp.stack([up_link.T.reshape(Q), down_link.T.reshape(Q)])
    level = occupation.astype(f32)
    raised = level.T + 1.0
    coef = jnp.stack(
        [
            (raised * coupling_re[:, None]).reshape(Q),
            (raised * coupling_im[:, None]).reshape(Q),
        ]
    )
    decay = jnp.sum(level * damping_rates[None, :], axis=1)
    big = ((2, M * A, 128), f32)
    sent = ((N * PIECES, 128), f32)
    listing = [((LIST, Q), f32), ((LIST, 128), f32)]
    dense, work = ((4, Q, 128), f32), ((M * A, 128), f32)

    state, send, listed, slots = call(
        open_kernel, [SMEM, VMEM, VMEM, VMEM], [big, sent] + listing, [dense, work]
    )(pigments, links, coef, density)

    def commutator(section, x):
        return call(
            functools.partial(commutator_kernel, section),
            [SMEM, SMEM, SMEM, VMEM, VMEM, VMEM],
            [big],
            [((256, 256), f32)],
        )(field, pulse_steps, decay, hamiltonian, dipole, x)[0]

    got = exchange(send)
    rate = commutator(0, state)
    middle, send = call(
        middle_kernel, [SMEM] + [VMEM] * 5, [big, sent], [dense, work]
    )(pigments, got, state, rate, listed, slots)
    got = exchange(send)
    rate = commutator(1, middle)
    out = call(
        close_kernel,
        [SMEM] + [VMEM] * 3,
        [((A, 2 * M * M), f32)],
        [big, dense, work],
    )(pigments, got, state, rate)
    return out[0]


def solution(mesh):
    rows = P("ha", None)
    return jax.shard_map(
        on_device,
        mesh=mesh,
        in_specs=(rows, rows, rows, rows) + (P(),) * 8,
        out_specs=rows,
        check_vma=False,
    )
```

```python
import functools
from typing import NamedTuple

import jax
import jax.numpy as jnp
from jax import lax
from jax.experimental import pallas as pl
from jax.experimental.pallas import tpu as pltpu
from jax.sharding import PartitionSpec as P

M = 96
K = 40
A = 32
N = 128
Q = A * K
ROWS = 97
LIST = 192
WIDE = 512
TAG = 96
CALL = 2048
PART = A // 4
HALF = 0.05
STEP = 0.1


class Size(NamedTuple):
    slots: int
    group: int
    forward: int
    few: int

    @property
    def relay(self):
        return self.group * self.forward

    @property
    def pieces(self):
        return 3 * self.slots + 1

    @property
    def factor(self):
        return -(-6 * self.few // 128) * 128


EVERY = Size(8, 8, 8, 8)
MOST = Size(4, 16, 8, 32)

f32, bf16, i32 = jnp.float32, jnp.bfloat16, jnp.int32
VMEM = pl.BlockSpec(memory_space=pltpu.VMEM)
SMEM = pl.BlockSpec(memory_space=pltpu.SMEM)
HBM = pl.BlockSpec(memory_space=pltpu.HBM)
NT = (((1,), (1,)), ((), ()))


def iota(shape, axis):
    return lax.broadcasted_iota(i32, shape, axis)


def dot(a, b):
    return jnp.dot(a, b, preferred_element_type=f32)


def dot_nt(a, b):
    return lax.dot_general(a, b, NT, preferred_element_type=f32)


def split(x):
    high = x.astype(bf16)
    return high, (x - high.astype(f32)).astype(bf16)


def pick(ones, x):
    high, low = split(x)
    return dot(ones, high) + dot(ones, low)


def onehot(mask):
    return jnp.where(mask, 1.0, 0.0).astype(bf16)


def shift(x, bits):
    return lax.shift_right_arithmetic(x, bits)


def widen(o0, o1, o2):
    lane = iota(o0.shape, 1)
    keep = lane < M
    t1 = pltpu.roll(jnp.where(lane >= 96, o0, o1), 32, 1)
    t2 = pltpu.roll(jnp.where(lane >= 64, o1, o2), 64, 1)
    t3 = pltpu.roll(o2, 96, 1)
    return [jnp.where(keep, t, 0.0) for t in (o0, t1, t2, t3)]


def narrow(t0, t1, t2, t3):
    lane = iota(t0.shape, 1)
    r1, r2, r3 = pltpu.roll(t1, 96, 1), pltpu.roll(t2, 64, 1), pltpu.roll(t3, 32, 1)
    return jnp.where(lane < 96, t0, r1), jnp.where(lane < 64, r1, r2), jnp.where(lane < 32, r2, r3)


def tile(x, j):
    return x[:, j * 128 : (j + 1) * 128]


def pigment_lanes(pig):
    lane = iota((1, 128), 1)
    at = jnp.concatenate([pig[...], jnp.full((1, 128 - K), -1, i32)], axis=1)
    again = pltpu.roll(at, K, 1) + 128
    return jnp.where(lane < K, at, jnp.where(lane < 2 * K, again, -1))


def pigment_rows(pig):
    at = jnp.broadcast_to(pigment_lanes(pig).astype(f32), (128, 128)).T[0 : 2 * K, 0:1]
    return jnp.where(iota((2 * K, 256), 1) == at.astype(i32), 1.0, 0.0)


def aux(ref, a):
    rows = pl.ds(a * ROWS, M)
    return jnp.concatenate([ref[0, rows, :], ref[1, rows, :]], axis=1)


def store_aux(ref, a, x):
    rows = pl.ds(a * ROWS, M)
    ref[0, rows, :] = x[:, 0:128]
    ref[1, rows, :] = x[:, 128:256]


def parts(source, target, sem):
    copies = []
    for j in range(A // PART):
        rows = pl.ds(j * PART * ROWS, PART * ROWS)
        copies.append(pltpu.make_async_copy(source.at[:, rows, :], target.at[:, rows, :], sem.at[j]))
    return copies


def plan(size, raw, listed, slots):
    flat = [jnp.zeros((8, 128), f32) for _ in range(5)]
    lane = iota((8, 128), 1)
    for b in range(16):
        piece = raw[pl.ds(b, 8, stride=16), :]
        first, at = divmod(b * K, 128)
        turned = pltpu.roll(piece, at, 1) if at else piece
        flat[first] = jnp.where((lane >= at) & (lane < at + K), turned, flat[first])
        if at + K > 128:
            flat[first + 1] = jnp.where(lane < at + K - 128, turned, flat[first + 1])
    flat = jnp.concatenate(flat, axis=1)
    before = onehot(iota((256, 256), 0) < iota((256, 256), 1))
    carry = jnp.zeros((N, 1), f32)
    facts = jnp.zeros((8, LIST), f32)
    for h in range(2):
        for g in range(2):
            row = slice(2 * h + g, 2 * h + g + 1)
            for low, width in ((0, 256), (256, 256), (512, 128)):
                span = slice(low, low + width)
                link = flat[row, span].astype(i32)
                dest = shift(link, 5)
                mine = dest == iota((N, width), 0)
                ones = jnp.where(mine, 1.0, 0.0)
                count = dot(ones.astype(bf16), before[0:width, 0:width]) + carry
                carry = count[:, width - 1 : width] + ones[:, width - 1 : width]
                rank = jnp.sum(jnp.where(mine, count, 0.0), axis=0, keepdims=True)
                place = jnp.sum(count, axis=0, keepdims=True).astype(i32)
                place = jnp.where(link >= 0, place, -1)
                item = iota((1, width), 1) + low
                mode = item - K * shift(item * 1639, 16)
                tag = ((link & 31) * K + mode + 1).astype(f32)
                if h == 0:
                    raised = flat[4 + g : 5 + g, span] + 1.0
                    sa, sb = raised * flat[6:7, span], raised * flat[7:8, span]
                else:
                    sa, sb = jnp.ones((1, width), f32), jnp.zeros((1, width), f32)
                here = onehot(iota((LIST, width), 0) == place)
                column = pl.ds(g * 640 + low, width)
                listed[:, column] = here if h == 0 else listed[:, column] + here
                fact = jnp.concatenate(
                    [rank, tag, sa, sb, dest.astype(f32), jnp.zeros((3, width), f32)], axis=0
                )
                high, low_part = split(fact)
                facts += dot_nt(high, here) + dot_nt(low_part, here)
    rank, tag, dest = facts[0:1], facts[1:2], facts[4:5]
    goal = dest.astype(i32)
    bits = size.group.bit_length() - 1
    me = lax.axis_index("ha")
    rows, columns = iota((N, N), 0), iota((N, N), 1)
    mate = shift(rows, bits) == shift(columns, bits)
    first = ((columns - me) & (size.group - 1)) < ((rows - me) & (size.group - 1))
    level = iota((N, 128), 1)
    free = onehot((carry <= level.astype(f32)) & (level < size.slots))
    here = dot(onehot(mate & first), free)
    whole = dot(onehot(mate), free)
    over = jnp.broadcast_to(jnp.maximum(carry - size.slots, 0.0), (N, 128)).astype(bf16)
    over_before = dot(onehot(mate & (columns < rows)), over)[:, 0:1]
    device = iota((N, LIST), 0)
    turn = jnp.sum(jnp.where(device == goal, over_before, 0.0), axis=0, keepdims=True) + rank - size.slots
    near = shift(device, bits) == shift(goal, bits)
    via_slot = jnp.full((N, LIST), -1.0, f32)
    ahead = jnp.zeros((N, 1), f32)
    for r in range(size.slots):
        hit = near & (carry <= r) & (here[:, r : r + 1] + ahead == turn)
        via_slot = jnp.where(hit, r * N + device.astype(f32), via_slot)
        ahead = ahead + whole[:, r : r + 1]
    via_slot = jnp.max(via_slot, axis=0, keepdims=True)
    past = rank >= size.slots
    lost = jnp.max(jnp.where(past & (via_slot < 0.0), 1.0, 0.0), axis=1, keepdims=True)
    slot = jnp.where(past, via_slot, rank * N + dest)
    slot = jnp.where(tag == 0.0, -1.0, slot)
    tag = jnp.where(past, tag + CALL * (1 + (goal & (size.group - 1))).astype(f32), tag)
    lost = jnp.broadcast_to(lost, (1, LIST))
    slots[...] = jnp.concatenate([slot, tag, facts[2:4], lost, jnp.zeros((3, LIST), f32)], axis=0)


def table_aux(x, rows, a, table):
    high, low = split(x)
    ones = rows[0:K, 0:M]
    row = dot(ones, high) + dot(ones, low)
    blank = jnp.zeros((128 - M, 256), bf16)
    high, low = jnp.concatenate([high, blank], axis=0), jnp.concatenate([low, blank], axis=0)
    column = dot_nt(rows, high) + dot_nt(rows, low)
    here = pl.ds(a * K, K)
    table[0, here, :] = row[:, 0:128]
    table[1, here, :] = row[:, 128:256]
    table[2, here, :] = column[0:K]
    table[3, here, :] = column[K : 2 * K]


def fill(size, table, listed, slots, lost, send):
    message = pick(listed[...], jnp.concatenate([table[j] for j in range(4)], axis=1))
    info = jnp.concatenate([slots[...], jnp.zeros((120, LIST), f32)], axis=0).T
    tag, sa, sb = info[:, 1:2], info[:, 2:3], info[:, 3:4]
    x0, x1, x2, x3 = (tile(message, j) for j in range(4))
    x0, x1, x2, x3 = sa * x1 + sb * x0, sb * x1 - sa * x0, sb * x2 - sa * x3, sa * x2 + sb * x3
    x0 = jnp.where(iota((LIST, 128), 1) == TAG, tag, x0)
    high, low = split(jnp.concatenate([x0, x1, x2, x3], axis=1))
    goal = slots[0:1, :].astype(i32)
    lane = iota((N, 128), 1)
    tags = jnp.where(lane == size.slots, lost, 0.0)
    for r in range(size.slots):
        ones = onehot(iota((N, LIST), 0) + r * N == goal)
        part = dot(ones, high) + dot(ones, low)
        tags = jnp.where(lane == r, pltpu.roll(tile(part, 0), (r - TAG) % 128, 1), tags)
        for j, piece in enumerate(narrow(*(tile(part, j) for j in range(4)))):
            send[pl.ds(3 * r + j, N, stride=size.pieces), :] = piece
    send[pl.ds(size.pieces - 1, N, stride=size.pieces), :] = tags


def open_kernel(
    size, pig, real, imaginary, up, down, level, density,
    out, send, listing, slots,
    state, listed, held, table, raw, leave, sem,
):
    copy = pltpu.make_async_copy(density, held, sem.at[0])
    copy.start()
    raw[...] = jnp.zeros((128, 128), f32)
    raw[0:32, 0:K] = up[...].astype(f32)
    raw[32:64, 0:K] = down[...].astype(f32)
    raw[64:96, 0:K] = level[...].astype(f32)
    raw[96:112, 0:K] = jnp.broadcast_to(real[...], (16, K))
    raw[112:128, 0:K] = jnp.broadcast_to(imaginary[...], (16, K))
    plan(size, raw, listed, slots)
    note = pltpu.make_async_copy(listed, listing, sem.at[1])
    note.start()
    rows = pigment_rows(pig).astype(bf16)
    copy.wait()
    for m in range(M // 2):
        pieces = widen(*(held[:, m * 384 + j * 128 : m * 384 + (j + 1) * 128] for j in range(3)))
        for j in range(2):
            for h in range(2):
                state[h, pl.ds(2 * m + j, A, stride=ROWS), :] = pieces[2 * j + h]
    give = parts(state, out, leave)
    for copy in give:
        copy.start()
    for a in range(A):
        table_aux(aux(state, a), rows, a, table)
    fill(size, table, listed, slots, jnp.zeros((1, 1), f32), send)
    note.wait()
    for copy in give:
        copy.wait()


def commutator_kernel(
    section, scale, field, steps, rates, level, hamiltonian, dipole, first, now,
    base, start, x, out, twice, arrive, also, leave,
):
    fetch, more = parts(now, x, arrive), parts(first, start, also)
    for copy in fetch + more:
        copy.start()
    h = hamiltonian[...] + field[steps[section]] * dipole[...]
    twice[...] = jnp.zeros((256, 256), f32)
    twice[0:M, 0:M] = h
    twice[128 : 128 + M, 128 : 128 + M] = h
    hh, hl = split(h)
    bh, bl = split(twice[...])
    decay = jnp.sum(level[...].astype(f32) * rates[...], axis=1, keepdims=True)
    give = parts(out, base, leave)
    for a in range(A):
        if a % PART == 0:
            fetch[a // PART].wait()
            more[a // PART].wait()
        y = aux(x, a)
        yh, yl = split(y)
        left = dot(hh, yh) + dot(hl, yh) + dot(hh, yl)
        right = dot(yh, bh) + dot(yh, bl) + dot(yl, bh)
        d = left - right
        d = jnp.concatenate([d[:, 128:256], -d[:, 0:128]], axis=1) - decay[a : a + 1, :] * y
        store_aux(out, a, aux(start, a) + scale * d)
        if a % PART == PART - 1:
            give[a // PART].start()
    for copy in give:
        copy.wait()


def receive_kernel(size, got, mine, relay, lost, high, low, ones):
    tags = got[pl.ds(size.pieces - 1, N, stride=size.pieces), :]
    across = tags.T[0:16, :].astype(i32)
    failed = jnp.max(across[size.slots : size.slots + 1], axis=1, keepdims=True)
    across = across[0 : size.slots]
    lane = iota((N, 128), 1)
    for r in range(size.slots):
        rows = pl.ds(r * N, N)
        t0, t1, t2, t3 = widen(*(got[pl.ds(3 * r + j, N, stride=size.pieces), :] for j in range(3)))
        t0 = jnp.where(lane == TAG, pltpu.roll(tags, TAG - r, 1), t0)
        for j, t in enumerate((t0, t1, t2, t3)):
            h, l = split(t)
            high[rows, j * 128 : (j + 1) * 128] = h
            low[rows, j * 128 : (j + 1) * 128] = l
    kinds = -(-(size.group + 1) // 8) * 8
    height = size.slots * kinds
    spread = [jnp.broadcast_to(across[r : r + 1], (kinds, N)) for r in range(size.slots)]
    spread = jnp.concatenate(spread, axis=0)
    kind = iota((height, N), 0) % kinds
    flags = (spread > 0) & (shift(spread, 11) == kind)
    ones_at = onehot(flags)
    before = onehot(iota((N, N), 0) < iota((N, N), 1))
    count = dot(ones_at, before)
    total = dot(ones_at, jnp.ones((N, N), bf16))
    rows, columns = iota((height, height), 0), iota((height, height), 1)
    earlier = onehot((rows % kinds == columns % kinds) & (columns < rows))
    count = count + dot(earlier, total.astype(bf16))
    member = count < jnp.where(kind == 0, LIST, size.forward).astype(f32)
    failed = jnp.maximum(failed, jnp.max(jnp.where(flags & ~member, 1.0, 0.0)).astype(i32))
    first = jnp.where(kind == 0, 0, LIST + (kind - 1) * size.forward)
    place = jnp.where(flags & member, count + first.astype(f32), -1.0)
    order = iota((LIST + size.relay, 128), 0)
    for r in range(size.slots):
        here = jnp.max(place[r * kinds : (r + 1) * kinds], axis=0, keepdims=True).astype(i32)
        ones[:, r * N : (r + 1) * N] = onehot(order == here)
    lost[...] = jnp.broadcast_to(failed, (8, 128))
    out = dot(ones[...], high[...]) + dot(ones[...], low[...])
    mine[...] = out[0:LIST]
    out = out[LIST:]
    called = CALL * (iota((size.relay, WIDE), 0) // size.forward + 1).astype(f32)
    mark = (iota((size.relay, WIDE), 1) == TAG) & (out > 0.0)
    relay[...] = out - jnp.where(mark, called, 0.0)


def clear(message, scale):
    return jnp.where((iota(message.shape, 1) & 127) < M, message * scale, 0.0)


def place_kernel(scale, pig, mine, base, out, total, dense, arrive, leave):
    fetch = parts(base, total, arrive)
    for copy in fetch:
        copy.start()
    rows = pigment_rows(pig)
    rowsb = rows.astype(bf16)
    rowst = jnp.concatenate([rows[0:K, 0:128], jnp.zeros((128 - K, 128), f32)], axis=0).T
    rowst = rowst[0:M, 0:K].astype(bf16)
    message = mine[...]
    tag = message[:, 0:128].T[TAG : TAG + 1, :].astype(i32)
    placed = pick(onehot(iota((Q, LIST), 0) + 1 == tag), clear(message, scale))
    for j in range(4):
        dense[j] = tile(placed, j)
    blank = jnp.zeros((128 - 2 * K, 128), f32)
    give = parts(total, out, leave)
    for a in range(A):
        if a % PART == 0:
            fetch[a // PART].wait()
        here = pl.ds(a * K, K)
        row = jnp.concatenate([dense[0, here, :], dense[1, here, :]], axis=1)
        high, low = split(row)
        new = dot(rowst, high) + dot(rowst, low)
        column = jnp.concatenate([dense[2, here, :], dense[3, here, :], blank], axis=0).T
        high, low = split(column[0:M, 0 : 2 * K])
        new = new + dot(high, rowsb) + dot(low, rowsb)
        store_aux(total, a, aux(total, a) + new)
        if a % PART == PART - 1:
            give[a // PART].start()
    for copy in give:
        copy.wait()


def few(size, pig, scale, relay):
    message = relay[...]
    head = message[:, 0:128]
    if size.relay < 128:
        head = jnp.concatenate([head, jnp.zeros((128 - size.relay, 128), f32)], axis=0)
    tag = head.T[TAG : TAG + 1, 0 : size.relay]
    flag = jnp.where(tag > 0.5, 1.0, 0.0)
    before = onehot(iota((size.relay, size.relay), 0) < iota((size.relay, size.relay), 1))
    place = dot(jnp.broadcast_to(flag, (8, size.relay)).astype(bf16), before)[0:1, :]
    place = jnp.where(tag > 0.5, place, -1.0).astype(i32)
    message = pick(onehot(iota((size.few, size.relay), 0) == place), message)
    tag = message[:, TAG : TAG + 1].astype(i32)
    message = clear(message, scale)
    who = shift((tag - 1) * 1639, 16)
    who = jnp.where(tag > 0, who, -1)
    mode = tag - 1 - who * K
    lane = iota((size.few, 128), 1)
    at = jnp.sum(jnp.where(lane == mode, pigment_lanes(pig), 0).astype(f32), axis=1, keepdims=True)
    at = at.astype(i32)
    ones = jnp.where(lane == at, 1.0, 0.0)
    zero = jnp.zeros((size.few, 128), f32)
    high = message.astype(bf16).astype(f32)
    low = message - high
    rest = size.factor - 6 * size.few
    left = [ones, ones, tile(high, 2), tile(low, 2), tile(high, 3), tile(low, 3), jnp.zeros((rest, 128), f32)]
    left = jnp.concatenate(left, axis=0)
    owner = jnp.concatenate([who.astype(f32)] * 6 + [jnp.full((rest, 1), -1.0, f32)], axis=0)
    left = jnp.where(iota((size.factor, 128), 1) == M, owner, left).T
    real = jnp.concatenate([ones, zero], axis=1)
    imaginary = jnp.concatenate([zero, ones], axis=1)
    right = [high[:, 0:256], low[:, 0:256], real, real, imaginary, imaginary, jnp.zeros((rest, 256), f32)]
    right = jnp.concatenate(right, axis=0)
    return left[0:M], left[M : M + 1].astype(i32), right.astype(bf16)


def add_few(ref, j, left, whom, right):
    span = range(j * PART, (j + 1) * PART)
    factors = jnp.concatenate([jnp.where(whom == a, left, 0.0).astype(bf16) for a in span], axis=0)
    new = dot(factors, right)
    for n, a in enumerate(span):
        store_aux(ref, a, aux(ref, a) + new[n * M : (n + 1) * M])


def middle_kernel(
    size, pig, relay, partial, listed, slots, lost, out, send, middle, table, chosen, arrive, leave, other
):
    fetch = parts(partial, middle, arrive)
    for copy in fetch:
        copy.start()
    choose = pltpu.make_async_copy(listed, chosen, other)
    choose.start()
    factors = few(size, pig, HALF, relay)
    rows = pigment_rows(pig).astype(bf16)
    give = parts(middle, out, leave)
    for j in range(A // PART):
        fetch[j].wait()
        add_few(middle, j, *factors)
        give[j].start()
        for a in range(j * PART, (j + 1) * PART):
            table_aux(aux(middle, a), rows, a, table)
    choose.wait()
    fill(size, table, chosen, slots, jnp.maximum(slots[4:5, 0:1], lost[0:1, 0:1].astype(f32)), send)
    for copy in give:
        copy.wait()


def close_kernel(size, pig, relay, partial, out, total, matrix, arrive, leave):
    fetch = parts(partial, total, arrive)
    for copy in fetch:
        copy.start()
    factors = few(size, pig, STEP, relay)
    give = []
    for j in range(A // PART):
        fetch[j].wait()
        add_few(total, j, *factors)
        span = pl.ds(j * PART, PART)
        for m in range(M // 2):
            pieces = []
            for i in range(2):
                for h in range(2):
                    pieces.append(total[h, pl.ds(j * PART * ROWS + 2 * m + i, PART, stride=ROWS), :])
            for i, piece in enumerate(narrow(*pieces)):
                matrix[span, m * 384 + i * 128 : m * 384 + (i + 1) * 128] = piece
        give.append(pltpu.make_async_copy(matrix.at[span, :], out.at[span, :], leave.at[j]))
        give[j].start()
    for copy in give:
        copy.wait()


def call(kernel, in_specs, outs, scratch, out_specs):
    return pl.pallas_call(
        kernel,
        in_specs=in_specs,
        out_specs=out_specs,
        out_shape=[jax.ShapeDtypeStruct(*o) for o in outs],
        scratch_shapes=[s if not isinstance(s, tuple) else pltpu.VMEM(*s) for s in scratch],
        compiler_params=pltpu.CompilerParams(vmem_limit_bytes=60 * 1024 * 1024),
    )


def on_device(
    density,
    up_link,
    down_link,
    occupation,
    pigments,
    hamiltonian,
    dipole,
    damping_rates,
    coupling_re,
    coupling_im,
    field,
    pulse_steps,
):
    big = ((2, A * ROWS, 128), f32)
    listing = ((LIST, Q), bf16)
    dense = ((4, Q, 128), f32)
    sems = pltpu.SemaphoreType.DMA((A // PART,))
    pig = pigments.reshape(1, K)

    def begin(size):
        return call(
            functools.partial(open_kernel, size),
            [VMEM] * 6 + [HBM],
            [big, ((N * size.pieces, 128), f32), listing, ((8, LIST), f32)],
            [
                big,
                listing,
                ((A, 2 * M * M), f32),
                dense,
                ((128, 128), f32),
                sems,
                pltpu.SemaphoreType.DMA((2,)),
            ],
            [HBM, VMEM, HBM, VMEM],
        )(
            pig,
            coupling_re.reshape(1, K),
            coupling_im.reshape(1, K),
            up_link,
            down_link,
            occupation,
            density,
        )

    def step(size, section, scale, state, x, send):
        got = lax.all_to_all(
            send.reshape(N, 1, size.pieces * 128), "ha", split_axis=0, concat_axis=0, tiled=True
        )
        base = call(
            functools.partial(commutator_kernel, section, scale),
            [SMEM, SMEM] + [VMEM] * 4 + [HBM] * 2,
            [big],
            [big, big, big, ((256, 256), f32), sems, sems, sems],
            [HBM],
        )(field, pulse_steps, damping_rates.reshape(1, K), occupation, hamiltonian, dipole, state, x)[0]
        got, base = lax.optimization_barrier((got, base))
        ahead = ((size.slots * N, WIDE), bf16)
        mine, relay, lost = call(
            functools.partial(receive_kernel, size),
            [VMEM],
            [((LIST, WIDE), f32), ((size.relay, WIDE), f32), ((8, 128), i32)],
            [ahead, ahead, ((LIST + size.relay, size.slots * N), bf16)],
            [VMEM, VMEM, VMEM],
        )(got.reshape(N * size.pieces, 128))
        relay = lax.all_to_all(
            relay.reshape(size.group, size.forward, WIDE),
            "ha",
            split_axis=0,
            concat_axis=0,
            tiled=True,
            axis_index_groups=[[i + j for j in range(size.group)] for i in range(0, N, size.group)],
        ).reshape(size.relay, WIDE)
        partial = call(
            functools.partial(place_kernel, scale),
            [VMEM, VMEM, HBM],
            [big],
            [big, dense, sems, sems],
            [HBM],
        )(pig, mine, base)[0]
        return relay, partial, lost

    def finish(size, state, relay, partial, lost, listed, slots):
        middle, send = call(
            functools.partial(middle_kernel, size),
            [VMEM, VMEM, HBM, HBM, VMEM, VMEM],
            [big, ((N * size.pieces, 128), f32)],
            [big, dense, listing, sems, sems, pltpu.SemaphoreType.DMA],
            [HBM, VMEM],
        )(pig, relay, partial, listed, slots, lost)
        relay, partial, lost = step(size, 1, STEP, state, middle, send)
        return call(
            functools.partial(close_kernel, size),
            [VMEM, VMEM, HBM],
            [((A, 2 * M * M), f32)],
            [big, ((A, 2 * M * M), f32), sems, sems],
            [HBM],
        )(pig, relay, partial)[0], lost[0, 0]

    state, send, listed, slots = begin(MOST)
    relay, partial, lost = step(MOST, 0, HALF, state, state, send)

    def again():
        state, send, listed, slots = begin(EVERY)
        relay, partial, lost = step(EVERY, 0, HALF, state, state, send)
        return finish(EVERY, state, relay, partial, lost, listed, slots)[0]

    out, lost = finish(MOST, state, relay, partial, lost, listed, slots)

    return lax.cond(lost > 0, again, lambda: out)


def solution(mesh):
    rows = P("ha", None)
    return jax.shard_map(
        on_device,
        mesh=mesh,
        in_specs=(rows, rows, rows, rows) + (P(),) * 8,
        out_specs=rows,
        check_vma=False,
    )
```

```python
import functools
from typing import NamedTuple

import jax
import jax.numpy as jnp
from jax import lax
from jax.experimental import pallas as pl
from jax.experimental.pallas import tpu as pltpu
from jax.sharding import PartitionSpec as P

M = 96
K = 40
A = 32
N = 128
Q = A * K
ROWS = 97
LIST = 192
WIDE = 512
TAG = 96
CALL = 2048
PART = A // 4
HALF = 0.05
STEP = 0.1


class Size(NamedTuple):
    slots: int
    group: int
    forward: int
    few: int
    unroll: int

    @property
    def relay(self):
        return self.group * self.forward

    @property
    def pieces(self):
        return 3 * self.slots + 1

    @property
    def factor(self):
        return -(-6 * self.few // 128) * 128


EVERY = Size(8, 8, 8, 8, 1)
MOST = Size(4, 16, 8, 32, 8)

f32, bf16, i32 = jnp.float32, jnp.bfloat16, jnp.int32
VMEM = pl.BlockSpec(memory_space=pltpu.VMEM)
SMEM = pl.BlockSpec(memory_space=pltpu.SMEM)
HBM = pl.BlockSpec(memory_space=pltpu.HBM)
NT = (((1,), (1,)), ((), ()))


def iota(shape, axis):
    return lax.broadcasted_iota(i32, shape, axis)


def dot(a, b):
    return jnp.dot(a, b, preferred_element_type=f32)


def dot_nt(a, b):
    return lax.dot_general(a, b, NT, preferred_element_type=f32)


def split(x):
    high = x.astype(bf16)
    return high, (x - high.astype(f32)).astype(bf16)


def pick(ones, x):
    high, low = split(x)
    return dot(ones, high) + dot(ones, low)


def onehot(mask):
    return jnp.where(mask, 1.0, 0.0).astype(bf16)


def shift(x, bits):
    return lax.shift_right_arithmetic(x, bits)


def widen(o0, o1, o2):
    lane = iota(o0.shape, 1)
    keep = lane < M
    t1 = pltpu.roll(jnp.where(lane >= 96, o0, o1), 32, 1)
    t2 = pltpu.roll(jnp.where(lane >= 64, o1, o2), 64, 1)
    t3 = pltpu.roll(o2, 96, 1)
    return [jnp.where(keep, t, 0.0) for t in (o0, t1, t2, t3)]


def narrow(t0, t1, t2, t3):
    lane = iota(t0.shape, 1)
    r1, r2, r3 = pltpu.roll(t1, 96, 1), pltpu.roll(t2, 64, 1), pltpu.roll(t3, 32, 1)
    return jnp.where(lane < 96, t0, r1), jnp.where(lane < 64, r1, r2), jnp.where(lane < 32, r2, r3)


def tile(x, j):
    return x[:, j * 128 : (j + 1) * 128]


def pigment_lanes(pig):
    lane = iota((1, 128), 1)
    at = jnp.concatenate([pig[...], jnp.full((1, 128 - K), -1, i32)], axis=1)
    again = pltpu.roll(at, K, 1) + 128
    return jnp.where(lane < K, at, jnp.where(lane < 2 * K, again, -1))


def pigment_rows(pig):
    at = jnp.broadcast_to(pigment_lanes(pig).astype(f32), (128, 128)).T[0 : 2 * K, 0:1]
    return jnp.where(iota((2 * K, 256), 1) == at.astype(i32), 1.0, 0.0)


def each(start, stop, unroll, body):
    def step(i, carry):
        body(i)
        return carry

    if unroll >= stop - start:
        for i in range(start, stop):
            body(i)
    else:
        lax.fori_loop(start, stop, step, 0, unroll=unroll)


def lanes(first):
    return pl.ds(pl.multiple_of(first, 128) if not isinstance(first, int) else first, 128)


def aux(ref, a):
    rows = pl.ds(a * ROWS, M)
    return jnp.concatenate([ref[0, rows, :], ref[1, rows, :]], axis=1)


def store_aux(ref, a, x):
    rows = pl.ds(a * ROWS, M)
    ref[0, rows, :] = x[:, 0:128]
    ref[1, rows, :] = x[:, 128:256]


def parts(source, target, sem):
    copies = []
    for j in range(A // PART):
        rows = pl.ds(j * PART * ROWS, PART * ROWS)
        copies.append(pltpu.make_async_copy(source.at[:, rows, :], target.at[:, rows, :], sem.at[j]))
    return copies


def plan(size, raw, listed, slots):
    flat = [jnp.zeros((8, 128), f32) for _ in range(5)]
    lane = iota((8, 128), 1)
    for b in range(16):
        piece = raw[pl.ds(b, 8, stride=16), :]
        first, at = divmod(b * K, 128)
        turned = pltpu.roll(piece, at, 1) if at else piece
        flat[first] = jnp.where((lane >= at) & (lane < at + K), turned, flat[first])
        if at + K > 128:
            flat[first + 1] = jnp.where(lane < at + K - 128, turned, flat[first + 1])
    flat = jnp.concatenate(flat, axis=1)
    before = onehot(iota((256, 256), 0) < iota((256, 256), 1))
    carry = jnp.zeros((N, 1), f32)
    facts = jnp.zeros((8, LIST), f32)
    for h in range(2):
        for g in range(2):
            row = slice(2 * h + g, 2 * h + g + 1)
            for low, width in ((0, 256), (256, 256), (512, 128)):
                span = slice(low, low + width)
                link = flat[row, span].astype(i32)
                dest = shift(link, 5)
                mine = dest == iota((N, width), 0)
                ones = jnp.where(mine, 1.0, 0.0)
                count = dot(ones.astype(bf16), before[0:width, 0:width]) + carry
                carry = count[:, width - 1 : width] + ones[:, width - 1 : width]
                rank = jnp.sum(jnp.where(mine, count, 0.0), axis=0, keepdims=True)
                place = jnp.sum(count, axis=0, keepdims=True).astype(i32)
                place = jnp.where(link >= 0, place, -1)
                item = iota((1, width), 1) + low
                mode = item - K * shift(item * 1639, 16)
                tag = ((link & 31) * K + mode + 1).astype(f32)
                if h == 0:
                    raised = flat[4 + g : 5 + g, span] + 1.0
                    sa, sb = raised * flat[6:7, span], raised * flat[7:8, span]
                else:
                    sa, sb = jnp.ones((1, width), f32), jnp.zeros((1, width), f32)
                here = onehot(iota((LIST, width), 0) == place)
                column = pl.ds(g * 640 + low, width)
                listed[:, column] = here if h == 0 else listed[:, column] + here
                fact = jnp.concatenate(
                    [rank, tag, sa, sb, dest.astype(f32), jnp.zeros((3, width), f32)], axis=0
                )
                high, low_part = split(fact)
                facts += dot_nt(high, here) + dot_nt(low_part, here)
    rank, tag, dest = facts[0:1], facts[1:2], facts[4:5]
    goal = dest.astype(i32)
    bits = size.group.bit_length() - 1
    me = lax.axis_index("ha")
    rows, columns = iota((N, N), 0), iota((N, N), 1)
    mate = shift(rows, bits) == shift(columns, bits)
    first = ((columns - me) & (size.group - 1)) < ((rows - me) & (size.group - 1))
    level = iota((N, 128), 1)
    free = onehot((carry <= level.astype(f32)) & (level < size.slots))
    here = dot(onehot(mate & first), free)
    whole = dot(onehot(mate), free)
    over = jnp.broadcast_to(jnp.maximum(carry - size.slots, 0.0), (N, 128)).astype(bf16)
    over_before = dot(onehot(mate & (columns < rows)), over)[:, 0:1]
    device = iota((N, LIST), 0)
    turn = jnp.sum(jnp.where(device == goal, over_before, 0.0), axis=0, keepdims=True) + rank - size.slots
    near = shift(device, bits) == shift(goal, bits)
    via_slot = jnp.full((N, LIST), -1.0, f32)
    ahead = jnp.zeros((N, 1), f32)
    for r in range(size.slots):
        hit = near & (carry <= r) & (here[:, r : r + 1] + ahead == turn)
        via_slot = jnp.where(hit, r * N + device.astype(f32), via_slot)
        ahead = ahead + whole[:, r : r + 1]
    via_slot = jnp.max(via_slot, axis=0, keepdims=True)
    past = rank >= size.slots
    lost = jnp.max(jnp.where(past & (via_slot < 0.0), 1.0, 0.0), axis=1, keepdims=True)
    slot = jnp.where(past, via_slot, rank * N + dest)
    slot = jnp.where(tag == 0.0, -1.0, slot)
    tag = jnp.where(past, tag + CALL * (1 + (goal & (size.group - 1))).astype(f32), tag)
    lost = jnp.broadcast_to(lost, (1, LIST))
    slots[...] = jnp.concatenate([slot, tag, facts[2:4], lost, jnp.zeros((3, LIST), f32)], axis=0)


def items(a):
    return pl.ds(a * K if isinstance(a, int) else pl.multiple_of(a * K, 8), K)


def table_aux(x, rows, a, table):
    high, low = split(x)
    ones = rows[0:K, 0:M]
    row = dot(ones, high) + dot(ones, low)
    blank = jnp.zeros((128 - M, 256), bf16)
    high, low = jnp.concatenate([high, blank], axis=0), jnp.concatenate([low, blank], axis=0)
    column = dot_nt(rows, high) + dot_nt(rows, low)
    here = items(a)
    table[0, here, :] = row[:, 0:128]
    table[1, here, :] = row[:, 128:256]
    table[2, here, :] = column[0:K]
    table[3, here, :] = column[K : 2 * K]


def fill(size, table, listed, slots, lost, send):
    message = pick(listed[...], jnp.concatenate([table[j] for j in range(4)], axis=1))
    info = jnp.concatenate([slots[...], jnp.zeros((120, LIST), f32)], axis=0).T
    tag, sa, sb = info[:, 1:2], info[:, 2:3], info[:, 3:4]
    x0, x1, x2, x3 = (tile(message, j) for j in range(4))
    x0, x1, x2, x3 = sa * x1 + sb * x0, sb * x1 - sa * x0, sb * x2 - sa * x3, sa * x2 + sb * x3
    x0 = jnp.where(iota((LIST, 128), 1) == TAG, tag, x0)
    high, low = split(jnp.concatenate([x0, x1, x2, x3], axis=1))
    goal = slots[0:1, :].astype(i32)
    lane = iota((N, 128), 1)
    tags = jnp.where(lane == size.slots, lost, 0.0)
    for r in range(size.slots):
        ones = onehot(iota((N, LIST), 0) + r * N == goal)
        part = dot(ones, high) + dot(ones, low)
        tags = jnp.where(lane == r, pltpu.roll(tile(part, 0), (r - TAG) % 128, 1), tags)
        for j, piece in enumerate(narrow(*(tile(part, j) for j in range(4)))):
            send[pl.ds(3 * r + j, N, stride=size.pieces), :] = piece
    send[pl.ds(size.pieces - 1, N, stride=size.pieces), :] = tags


def open_kernel(
    size, pig, real, imaginary, up, down, level, density,
    out, send, listing, slots,
    state, listed, held, table, raw, leave, sem,
):
    copy = pltpu.make_async_copy(density, held, sem.at[0])
    copy.start()
    raw[...] = jnp.zeros((128, 128), f32)
    raw[0:32, 0:K] = up[...].astype(f32)
    raw[32:64, 0:K] = down[...].astype(f32)
    raw[64:96, 0:K] = level[...].astype(f32)
    raw[96:112, 0:K] = jnp.broadcast_to(real[...], (16, K))
    raw[112:128, 0:K] = jnp.broadcast_to(imaginary[...], (16, K))
    plan(size, raw, listed, slots)
    note = pltpu.make_async_copy(listed, listing, sem.at[1])
    note.start()
    rows = pigment_rows(pig).astype(bf16)
    copy.wait()

    def unfold(m):
        pieces = widen(*(held[:, lanes(m * 384 + j * 128)] for j in range(3)))
        for j in range(2):
            for h in range(2):
                state[h, pl.ds(2 * m + j, A, stride=ROWS), :] = pieces[2 * j + h]

    each(0, M // 2, size.unroll, unfold)
    give = parts(state, out, leave)
    for copy in give:
        copy.start()
    each(0, A, size.unroll, lambda a: table_aux(aux(state, a), rows, a, table))
    fill(size, table, listed, slots, jnp.zeros((1, 1), f32), send)
    note.wait()
    for copy in give:
        copy.wait()


def commutator_kernel(
    unroll, section, scale, field, steps, rates, level, hamiltonian, dipole, first, now,
    base, start, x, out, twice, fading, arrive, also, leave,
):
    fetch, more = parts(now, x, arrive), parts(first, start, also)
    for copy in fetch + more:
        copy.start()
    h = hamiltonian[...] + field[steps[section]] * dipole[...]
    twice[...] = jnp.zeros((256, 256), f32)
    twice[0:M, 0:M] = h
    twice[128 : 128 + M, 128 : 128 + M] = h
    hh, hl = split(h)
    bh, bl = split(twice[...])
    decay = jnp.sum(level[...].astype(f32) * rates[...], axis=1, keepdims=True)
    fading[...] = jnp.broadcast_to(decay, (A, 128))
    give = parts(out, base, leave)

    def one(a):
        y = aux(x, a)
        yh, yl = split(y)
        left = dot(hh, yh) + dot(hl, yh) + dot(hh, yl)
        right = dot(yh, bh) + dot(yh, bl) + dot(yl, bh)
        d = left - right
        d = jnp.concatenate([d[:, 128:256], -d[:, 0:128]], axis=1) - fading[pl.ds(a, 1), 0:1] * y
        store_aux(out, a, aux(start, a) + scale * d)

    for j in range(A // PART):
        fetch[j].wait()
        more[j].wait()
        each(j * PART, (j + 1) * PART, unroll, one)
        give[j].start()
    for copy in give:
        copy.wait()


def receive_kernel(size, got, mine, relay, lost, high, low, ones):
    tags = got[pl.ds(size.pieces - 1, N, stride=size.pieces), :]
    across = tags.T[0:16, :].astype(i32)
    failed = jnp.max(across[size.slots : size.slots + 1], axis=1, keepdims=True)
    across = across[0 : size.slots]
    lane = iota((N, 128), 1)
    for r in range(size.slots):
        rows = pl.ds(r * N, N)
        t0, t1, t2, t3 = widen(*(got[pl.ds(3 * r + j, N, stride=size.pieces), :] for j in range(3)))
        t0 = jnp.where(lane == TAG, pltpu.roll(tags, TAG - r, 1), t0)
        for j, t in enumerate((t0, t1, t2, t3)):
            h, l = split(t)
            high[rows, j * 128 : (j + 1) * 128] = h
            low[rows, j * 128 : (j + 1) * 128] = l
    kinds = -(-(size.group + 1) // 8) * 8
    height = size.slots * kinds
    spread = [jnp.broadcast_to(across[r : r + 1], (kinds, N)) for r in range(size.slots)]
    spread = jnp.concatenate(spread, axis=0)
    kind = iota((height, N), 0) % kinds
    flags = (spread > 0) & (shift(spread, 11) == kind)
    ones_at = onehot(flags)
    before = onehot(iota((N, N), 0) < iota((N, N), 1))
    count = dot(ones_at, before)
    total = dot(ones_at, jnp.ones((N, N), bf16))
    rows, columns = iota((height, height), 0), iota((height, height), 1)
    earlier = onehot((rows % kinds == columns % kinds) & (columns < rows))
    count = count + dot(earlier, total.astype(bf16))
    member = count < jnp.where(kind == 0, LIST, size.forward).astype(f32)
    failed = jnp.maximum(failed, jnp.max(jnp.where(flags & ~member, 1.0, 0.0)).astype(i32))
    first = jnp.where(kind == 0, 0, LIST + (kind - 1) * size.forward)
    place = jnp.where(flags & member, count + first.astype(f32), -1.0)
    order = iota((LIST + size.relay, 128), 0)
    for r in range(size.slots):
        here = jnp.max(place[r * kinds : (r + 1) * kinds], axis=0, keepdims=True).astype(i32)
        ones[:, r * N : (r + 1) * N] = onehot(order == here)
    lost[...] = jnp.broadcast_to(failed, (8, 128))
    out = dot(ones[...], high[...]) + dot(ones[...], low[...])
    mine[...] = out[0:LIST]
    out = out[LIST:]
    called = CALL * (iota((size.relay, WIDE), 0) // size.forward + 1).astype(f32)
    mark = (iota((size.relay, WIDE), 1) == TAG) & (out > 0.0)
    relay[...] = out - jnp.where(mark, called, 0.0)


def clear(message, scale):
    return jnp.where((iota(message.shape, 1) & 127) < M, message * scale, 0.0)


def place_kernel(unroll, scale, pig, mine, base, out, total, dense, arrive, leave):
    fetch = parts(base, total, arrive)
    for copy in fetch:
        copy.start()
    rows = pigment_rows(pig)
    rowsb = rows.astype(bf16)
    rowst = jnp.concatenate([rows[0:K, 0:128], jnp.zeros((128 - K, 128), f32)], axis=0).T
    rowst = rowst[0:M, 0:K].astype(bf16)
    message = mine[...]
    tag = message[:, 0:128].T[TAG : TAG + 1, :].astype(i32)
    placed = pick(onehot(iota((Q, LIST), 0) + 1 == tag), clear(message, scale))
    for j in range(4):
        dense[j] = tile(placed, j)
    blank = jnp.zeros((128 - 2 * K, 128), f32)
    give = parts(total, out, leave)

    def one(a):
        here = items(a)
        row = jnp.concatenate([dense[0, here, :], dense[1, here, :]], axis=1)
        high, low = split(row)
        new = dot(rowst, high) + dot(rowst, low)
        column = jnp.concatenate([dense[2, here, :], dense[3, here, :], blank], axis=0).T
        high, low = split(column[0:M, 0 : 2 * K])
        new = new + dot(high, rowsb) + dot(low, rowsb)
        store_aux(total, a, aux(total, a) + new)

    for j in range(A // PART):
        fetch[j].wait()
        each(j * PART, (j + 1) * PART, unroll, one)
        give[j].start()
    for copy in give:
        copy.wait()


def few(size, pig, scale, relay):
    message = relay[...]
    head = message[:, 0:128]
    if size.relay < 128:
        head = jnp.concatenate([head, jnp.zeros((128 - size.relay, 128), f32)], axis=0)
    tag = head.T[TAG : TAG + 1, 0 : size.relay]
    flag = jnp.where(tag > 0.5, 1.0, 0.0)
    before = onehot(iota((size.relay, size.relay), 0) < iota((size.relay, size.relay), 1))
    place = dot(jnp.broadcast_to(flag, (8, size.relay)).astype(bf16), before)[0:1, :]
    place = jnp.where(tag > 0.5, place, -1.0).astype(i32)
    message = pick(onehot(iota((size.few, size.relay), 0) == place), message)
    tag = message[:, TAG : TAG + 1].astype(i32)
    message = clear(message, scale)
    who = shift((tag - 1) * 1639, 16)
    who = jnp.where(tag > 0, who, -1)
    mode = tag - 1 - who * K
    lane = iota((size.few, 128), 1)
    at = jnp.sum(jnp.where(lane == mode, pigment_lanes(pig), 0).astype(f32), axis=1, keepdims=True)
    at = at.astype(i32)
    ones = jnp.where(lane == at, 1.0, 0.0)
    zero = jnp.zeros((size.few, 128), f32)
    high = message.astype(bf16).astype(f32)
    low = message - high
    rest = size.factor - 6 * size.few
    left = [ones, ones, tile(high, 2), tile(low, 2), tile(high, 3), tile(low, 3), jnp.zeros((rest, 128), f32)]
    left = jnp.concatenate(left, axis=0)
    owner = jnp.concatenate([who.astype(f32)] * 6 + [jnp.full((rest, 1), -1.0, f32)], axis=0)
    left = jnp.where(iota((size.factor, 128), 1) == M, owner, left).T
    real = jnp.concatenate([ones, zero], axis=1)
    imaginary = jnp.concatenate([zero, ones], axis=1)
    right = [high[:, 0:256], low[:, 0:256], real, real, imaginary, imaginary, jnp.zeros((rest, 256), f32)]
    right = jnp.concatenate(right, axis=0)
    return left[0:M], left[M : M + 1].astype(i32), right.astype(bf16)


def add_few(ref, j, left, whom, right):
    span = range(j * PART, (j + 1) * PART)
    factors = jnp.concatenate([jnp.where(whom == a, left, 0.0).astype(bf16) for a in span], axis=0)
    new = dot(factors, right)
    for n, a in enumerate(span):
        store_aux(ref, a, aux(ref, a) + new[n * M : (n + 1) * M])


def middle_kernel(
    size, pig, relay, partial, listed, slots, lost, out, send, middle, table, chosen, arrive, leave, other
):
    fetch = parts(partial, middle, arrive)
    for copy in fetch:
        copy.start()
    choose = pltpu.make_async_copy(listed, chosen, other)
    choose.start()
    factors = few(size, pig, HALF, relay)
    rows = pigment_rows(pig).astype(bf16)
    give = parts(middle, out, leave)
    for j in range(A // PART):
        fetch[j].wait()
        add_few(middle, j, *factors)
        give[j].start()
        each(j * PART, (j + 1) * PART, size.unroll, lambda a: table_aux(aux(middle, a), rows, a, table))
    choose.wait()
    fill(size, table, chosen, slots, jnp.maximum(slots[4:5, 0:1], lost[0:1, 0:1].astype(f32)), send)
    for copy in give:
        copy.wait()


def close_kernel(size, pig, relay, partial, out, total, matrix, arrive, leave):
    fetch = parts(partial, total, arrive)
    for copy in fetch:
        copy.start()
    factors = few(size, pig, STEP, relay)
    give = []
    for j in range(A // PART):
        fetch[j].wait()
        add_few(total, j, *factors)
        span = pl.ds(j * PART, PART)

        def fold(m):
            pieces = []
            for i in range(2):
                for h in range(2):
                    pieces.append(total[h, pl.ds(j * PART * ROWS + 2 * m + i, PART, stride=ROWS), :])
            for i, piece in enumerate(narrow(*pieces)):
                matrix[span, lanes(m * 384 + i * 128)] = piece

        each(0, M // 2, size.unroll, fold)
        give.append(pltpu.make_async_copy(matrix.at[span, :], out.at[span, :], leave.at[j]))
        give[j].start()
    for copy in give:
        copy.wait()


def call(kernel, in_specs, outs, scratch, out_specs):
    return pl.pallas_call(
        kernel,
        in_specs=in_specs,
        out_specs=out_specs,
        out_shape=[jax.ShapeDtypeStruct(*o) for o in outs],
        scratch_shapes=[s if not isinstance(s, tuple) else pltpu.VMEM(*s) for s in scratch],
        compiler_params=pltpu.CompilerParams(vmem_limit_bytes=60 * 1024 * 1024),
    )


def on_device(
    density,
    up_link,
    down_link,
    occupation,
    pigments,
    hamiltonian,
    dipole,
    damping_rates,
    coupling_re,
    coupling_im,
    field,
    pulse_steps,
):
    big = ((2, A * ROWS, 128), f32)
    listing = ((LIST, Q), bf16)
    dense = ((4, Q, 128), f32)
    sems = pltpu.SemaphoreType.DMA((A // PART,))
    pig = pigments.reshape(1, K)

    def begin(size):
        return call(
            functools.partial(open_kernel, size),
            [VMEM] * 6 + [HBM],
            [big, ((N * size.pieces, 128), f32), listing, ((8, LIST), f32)],
            [
                big,
                listing,
                ((A, 2 * M * M), f32),
                dense,
                ((128, 128), f32),
                sems,
                pltpu.SemaphoreType.DMA((2,)),
            ],
            [HBM, VMEM, HBM, VMEM],
        )(
            pig,
            coupling_re.reshape(1, K),
            coupling_im.reshape(1, K),
            up_link,
            down_link,
            occupation,
            density,
        )

    def step(size, section, scale, state, x, send):
        got = lax.all_to_all(
            send.reshape(N, 1, size.pieces * 128), "ha", split_axis=0, concat_axis=0, tiled=True
        )
        base = call(
            functools.partial(commutator_kernel, min(size.unroll, 2), section, scale),
            [SMEM, SMEM] + [VMEM] * 4 + [HBM] * 2,
            [big],
            [big, big, big, ((256, 256), f32), ((A, 128), f32), sems, sems, sems],
            [HBM],
        )(field, pulse_steps, damping_rates.reshape(1, K), occupation, hamiltonian, dipole, state, x)[0]
        got, base = lax.optimization_barrier((got, base))
        ahead = ((size.slots * N, WIDE), bf16)
        mine, relay, lost = call(
            functools.partial(receive_kernel, size),
            [VMEM],
            [((LIST, WIDE), f32), ((size.relay, WIDE), f32), ((8, 128), i32)],
            [ahead, ahead, ((LIST + size.relay, size.slots * N), bf16)],
            [VMEM, VMEM, VMEM],
        )(got.reshape(N * size.pieces, 128))
        relay = lax.all_to_all(
            relay.reshape(size.group, size.forward, WIDE),
            "ha",
            split_axis=0,
            concat_axis=0,
            tiled=True,
            axis_index_groups=[[i + j for j in range(size.group)] for i in range(0, N, size.group)],
        ).reshape(size.relay, WIDE)
        partial = call(
            functools.partial(place_kernel, min(size.unroll, 8), scale),
            [VMEM, VMEM, HBM],
            [big],
            [big, dense, sems, sems],
            [HBM],
        )(pig, mine, base)[0]
        return relay, partial, lost

    def finish(size, state, relay, partial, lost, listed, slots):
        middle, send = call(
            functools.partial(middle_kernel, size),
            [VMEM, VMEM, HBM, HBM, VMEM, VMEM],
            [big, ((N * size.pieces, 128), f32)],
            [big, dense, listing, sems, sems, pltpu.SemaphoreType.DMA],
            [HBM, VMEM],
        )(pig, relay, partial, listed, slots, lost)
        relay, partial, lost = step(size, 1, STEP, state, middle, send)
        return call(
            functools.partial(close_kernel, size),
            [VMEM, VMEM, HBM],
            [((A, 2 * M * M), f32)],
            [big, ((A, 2 * M * M), f32), sems, sems],
            [HBM],
        )(pig, relay, partial)[0], lost[0, 0]

    state, send, listed, slots = begin(MOST)
    relay, partial, lost = step(MOST, 0, HALF, state, state, send)

    def again():
        state, send, listed, slots = begin(EVERY)
        relay, partial, lost = step(EVERY, 0, HALF, state, state, send)
        return finish(EVERY, state, relay, partial, lost, listed, slots)[0]

    out, lost = finish(MOST, state, relay, partial, lost, listed, slots)

    return lax.cond(lost > 0, again, lambda: out)


def solution(mesh):
    rows = P("ha", None)
    return jax.shard_map(
        on_device,
        mesh=mesh,
        in_specs=(rows, rows, rows, rows) + (P(),) * 8,
        out_specs=rows,
        check_vma=False,
    )
```

```python
import functools
from typing import NamedTuple

import jax
import jax.numpy as jnp
from jax import lax
from jax.experimental import pallas as pl
from jax.experimental.pallas import tpu as pltpu
from jax.sharding import PartitionSpec as P

M = 96
K = 40
A = 32
N = 128
Q = A * K
ROWS = 97
LIST = 192
WIDE = 512
TAG = 96
CALL = 2048
PART = A // 4
HALF = 0.05
STEP = 0.1


class Size(NamedTuple):
    slots: int
    group: int
    forward: int
    few: int
    unroll: int

    @property
    def relay(self):
        return self.group * self.forward

    @property
    def pieces(self):
        return 3 * self.slots + 1

    @property
    def factor(self):
        return -(-6 * self.few // 128) * 128


EVERY = Size(8, 8, 8, 8, 1)
MOST = Size(4, 16, 8, 32, 8)

f32, bf16, i32 = jnp.float32, jnp.bfloat16, jnp.int32
VMEM = pl.BlockSpec(memory_space=pltpu.VMEM)
SMEM = pl.BlockSpec(memory_space=pltpu.SMEM)
HBM = pl.BlockSpec(memory_space=pltpu.HBM)
NT = (((1,), (1,)), ((), ()))


def iota(shape, axis):
    return lax.broadcasted_iota(i32, shape, axis)


def dot(a, b):
    return jnp.dot(a, b, preferred_element_type=f32)


def dot_nt(a, b):
    return lax.dot_general(a, b, NT, preferred_element_type=f32)


def split(x):
    high = x.astype(bf16)
    return high, (x - high.astype(f32)).astype(bf16)


def pick(ones, x):
    high, low = split(x)
    return dot(ones, high) + dot(ones, low)


def onehot(mask):
    return jnp.where(mask, 1.0, 0.0).astype(bf16)


def shift(x, bits):
    return lax.shift_right_arithmetic(x, bits)


def widen(o0, o1, o2):
    lane = iota(o0.shape, 1)
    keep = lane < M
    t1 = pltpu.roll(jnp.where(lane >= 96, o0, o1), 32, 1)
    t2 = pltpu.roll(jnp.where(lane >= 64, o1, o2), 64, 1)
    t3 = pltpu.roll(o2, 96, 1)
    return [jnp.where(keep, t, 0.0) for t in (o0, t1, t2, t3)]


def narrow(t0, t1, t2, t3):
    lane = iota(t0.shape, 1)
    r1, r2, r3 = pltpu.roll(t1, 96, 1), pltpu.roll(t2, 64, 1), pltpu.roll(t3, 32, 1)
    return jnp.where(lane < 96, t0, r1), jnp.where(lane < 64, r1, r2), jnp.where(lane < 32, r2, r3)


def tile(x, j):
    return x[:, j * 128 : (j + 1) * 128]


def pigment_lanes(pig):
    lane = iota((1, 128), 1)
    at = jnp.concatenate([pig[...], jnp.full((1, 128 - K), -1, i32)], axis=1)
    again = pltpu.roll(at, K, 1) + 128
    return jnp.where(lane < K, at, jnp.where(lane < 2 * K, again, -1))


def pigment_rows(pig):
    at = jnp.broadcast_to(pigment_lanes(pig).astype(f32), (128, 128)).T[0 : 2 * K, 0:1]
    return jnp.where(iota((2 * K, 256), 1) == at.astype(i32), 1.0, 0.0)


def each(start, stop, unroll, body):
    def step(i, carry):
        body(i)
        return carry

    if unroll >= stop - start:
        for i in range(start, stop):
            body(i)
    else:
        lax.fori_loop(start, stop, step, 0, unroll=unroll)


def lanes(first):
    return pl.ds(pl.multiple_of(first, 128) if not isinstance(first, int) else first, 128)


def aux(ref, a):
    rows = pl.ds(a * ROWS, M)
    return jnp.concatenate([ref[0, rows, :], ref[1, rows, :]], axis=1)


def store_aux(ref, a, x):
    rows = pl.ds(a * ROWS, M)
    ref[0, rows, :] = x[:, 0:128]
    ref[1, rows, :] = x[:, 128:256]


def parts(source, target, sem):
    copies = []
    for j in range(A // PART):
        rows = pl.ds(j * PART * ROWS, PART * ROWS)
        copies.append(pltpu.make_async_copy(source.at[:, rows, :], target.at[:, rows, :], sem.at[j]))
    return copies


def plan(size, raw, listed, slots):
    flat = [jnp.zeros((8, 128), f32) for _ in range(5)]
    lane = iota((8, 128), 1)
    for b in range(16):
        piece = raw[pl.ds(b, 8, stride=16), :]
        first, at = divmod(b * K, 128)
        turned = pltpu.roll(piece, at, 1) if at else piece
        flat[first] = jnp.where((lane >= at) & (lane < at + K), turned, flat[first])
        if at + K > 128:
            flat[first + 1] = jnp.where(lane < at + K - 128, turned, flat[first + 1])
    flat = jnp.concatenate(flat, axis=1)
    before = onehot(iota((256, 256), 0) < iota((256, 256), 1))
    carry = jnp.zeros((N, 1), f32)
    facts = jnp.zeros((8, LIST), f32)
    for h in range(2):
        for g in range(2):
            row = slice(2 * h + g, 2 * h + g + 1)
            for low, width in ((0, 256), (256, 256), (512, 128)):
                span = slice(low, low + width)
                link = flat[row, span].astype(i32)
                dest = shift(link, 5)
                mine = dest == iota((N, width), 0)
                ones = jnp.where(mine, 1.0, 0.0)
                count = dot(ones.astype(bf16), before[0:width, 0:width]) + carry
                carry = count[:, width - 1 : width] + ones[:, width - 1 : width]
                rank = jnp.sum(jnp.where(mine, count, 0.0), axis=0, keepdims=True)
                place = jnp.sum(count, axis=0, keepdims=True).astype(i32)
                place = jnp.where(link >= 0, place, -1)
                item = iota((1, width), 1) + low
                mode = item - K * shift(item * 1639, 16)
                tag = ((link & 31) * K + mode + 1).astype(f32)
                if h == 0:
                    raised = flat[4 + g : 5 + g, span] + 1.0
                    sa, sb = raised * flat[6:7, span], raised * flat[7:8, span]
                else:
                    sa, sb = jnp.ones((1, width), f32), jnp.zeros((1, width), f32)
                here = onehot(iota((LIST, width), 0) == place)
                column = pl.ds(g * 640 + low, width)
                listed[:, column] = here if h == 0 else listed[:, column] + here
                fact = jnp.concatenate(
                    [rank, tag, sa, sb, dest.astype(f32), jnp.zeros((3, width), f32)], axis=0
                )
                high, low_part = split(fact)
                facts += dot_nt(high, here) + dot_nt(low_part, here)
    rank, tag, dest = facts[0:1], facts[1:2], facts[4:5]
    goal = dest.astype(i32)
    bits = size.group.bit_length() - 1
    me = lax.axis_index("ha")
    rows, columns = iota((N, N), 0), iota((N, N), 1)
    mate = shift(rows, bits) == shift(columns, bits)
    first = ((columns - me) & (size.group - 1)) < ((rows - me) & (size.group - 1))
    level = iota((N, 128), 1)
    free = onehot((carry <= level.astype(f32)) & (level < size.slots))
    here = dot(onehot(mate & first), free)
    whole = dot(onehot(mate), free)
    over = jnp.broadcast_to(jnp.maximum(carry - size.slots, 0.0), (N, 128)).astype(bf16)
    over_before = dot(onehot(mate & (columns < rows)), over)[:, 0:1]
    device = iota((N, LIST), 0)
    turn = jnp.sum(jnp.where(device == goal, over_before, 0.0), axis=0, keepdims=True) + rank - size.slots
    near = shift(device, bits) == shift(goal, bits)
    via_slot = jnp.full((N, LIST), -1.0, f32)
    ahead = jnp.zeros((N, 1), f32)
    for r in range(size.slots):
        hit = near & (carry <= r) & (here[:, r : r + 1] + ahead == turn)
        via_slot = jnp.where(hit, r * N + device.astype(f32), via_slot)
        ahead = ahead + whole[:, r : r + 1]
    via_slot = jnp.max(via_slot, axis=0, keepdims=True)
    past = rank >= size.slots
    lost = jnp.max(jnp.where(past & (via_slot < 0.0), 1.0, 0.0), axis=1, keepdims=True)
    slot = jnp.where(past, via_slot, rank * N + dest)
    slot = jnp.where(tag == 0.0, -1.0, slot)
    tag = jnp.where(past, tag + CALL * (1 + (goal & (size.group - 1))).astype(f32), tag)
    lost = jnp.broadcast_to(lost, (1, LIST))
    slots[...] = jnp.concatenate([slot, tag, facts[2:4], lost, jnp.zeros((3, LIST), f32)], axis=0)


def items(a):
    return pl.ds(a * K if isinstance(a, int) else pl.multiple_of(a * K, 8), K)


def table_aux(x, rows, a, table):
    high, low = split(x)
    ones = rows[0:K, 0:M]
    row = dot(ones, high) + dot(ones, low)
    blank = jnp.zeros((128 - M, 256), bf16)
    high, low = jnp.concatenate([high, blank], axis=0), jnp.concatenate([low, blank], axis=0)
    column = dot_nt(rows, high) + dot_nt(rows, low)
    here = items(a)
    table[0, here, :] = row[:, 0:128]
    table[1, here, :] = row[:, 128:256]
    table[2, here, :] = column[0:K]
    table[3, here, :] = column[K : 2 * K]


def fill(size, table, listed, slots, lost, send):
    message = pick(listed[...], jnp.concatenate([table[j] for j in range(4)], axis=1))
    info = jnp.concatenate([slots[...], jnp.zeros((120, LIST), f32)], axis=0).T
    tag, sa, sb = info[:, 1:2], info[:, 2:3], info[:, 3:4]
    x0, x1, x2, x3 = (tile(message, j) for j in range(4))
    x0, x1, x2, x3 = sa * x1 + sb * x0, sb * x1 - sa * x0, sb * x2 - sa * x3, sa * x2 + sb * x3
    x0 = jnp.where(iota((LIST, 128), 1) == TAG, tag, x0)
    high, low = split(jnp.concatenate([x0, x1, x2, x3], axis=1))
    goal = slots[0:1, :].astype(i32)
    lane = iota((N, 128), 1)
    tags = jnp.where(lane == size.slots, lost, 0.0)
    for r in range(size.slots):
        ones = onehot(iota((N, LIST), 0) + r * N == goal)
        part = dot(ones, high) + dot(ones, low)
        tags = jnp.where(lane == r, pltpu.roll(tile(part, 0), (r - TAG) % 128, 1), tags)
        for j, piece in enumerate(narrow(*(tile(part, j) for j in range(4)))):
            send[pl.ds(3 * r + j, N, stride=size.pieces), :] = piece
    send[pl.ds(size.pieces - 1, N, stride=size.pieces), :] = tags


def open_kernel(
    size, pig, real, imaginary, up, down, level, density,
    out, send, listing, slots,
    state, listed, held, table, raw, leave, sem,
):
    copy = pltpu.make_async_copy(density, held, sem.at[0])
    copy.start()
    raw[...] = jnp.zeros((128, 128), f32)
    raw[0:32, 0:K] = up[...].astype(f32)
    raw[32:64, 0:K] = down[...].astype(f32)
    raw[64:96, 0:K] = level[...].astype(f32)
    raw[96:112, 0:K] = jnp.broadcast_to(real[...], (16, K))
    raw[112:128, 0:K] = jnp.broadcast_to(imaginary[...], (16, K))
    plan(size, raw, listed, slots)
    note = pltpu.make_async_copy(listed, listing, sem.at[1])
    note.start()
    rows = pigment_rows(pig).astype(bf16)
    copy.wait()

    def unfold(m):
        pieces = widen(*(held[:, lanes(m * 384 + j * 128)] for j in range(3)))
        for j in range(2):
            for h in range(2):
                state[h, pl.ds(2 * m + j, A, stride=ROWS), :] = pieces[2 * j + h]

    each(0, M // 2, size.unroll * 6, unfold)
    give = parts(state, out, leave)
    for copy in give:
        copy.start()
    each(0, A, size.unroll, lambda a: table_aux(aux(state, a), rows, a, table))
    fill(size, table, listed, slots, jnp.zeros((1, 1), f32), send)
    note.wait()
    for copy in give:
        copy.wait()


def commutator_kernel(
    unroll, section, scale, field, steps, rates, level, hamiltonian, dipole, first, now,
    base, start, x, out, twice, fading, arrive, also, leave,
):
    fetch, more = parts(now, x, arrive), parts(first, start, also)
    for copy in fetch + more:
        copy.start()
    h = hamiltonian[...] + field[steps[section]] * dipole[...]
    twice[...] = jnp.zeros((256, 256), f32)
    twice[0:M, 0:M] = h
    twice[128 : 128 + M, 128 : 128 + M] = h
    hh, hl = split(h)
    bh, bl = split(twice[...])
    decay = jnp.sum(level[...].astype(f32) * rates[...], axis=1, keepdims=True)
    fading[...] = jnp.broadcast_to(decay, (A, 128))
    give = parts(out, base, leave)

    def one(a):
        y = aux(x, a)
        yh, yl = split(y)
        left = dot(hh, yh) + dot(hl, yh) + dot(hh, yl)
        right = dot(yh, bh) + dot(yh, bl) + dot(yl, bh)
        d = left - right
        d = jnp.concatenate([d[:, 128:256], -d[:, 0:128]], axis=1) - fading[pl.ds(a, 1), 0:1] * y
        store_aux(out, a, aux(start, a) + scale * d)

    for j in range(A // PART):
        fetch[j].wait()
        more[j].wait()
        each(j * PART, (j + 1) * PART, unroll, one)
        give[j].start()
    for copy in give:
        copy.wait()


def receive_kernel(size, got, mine, relay, lost, high, low, ones):
    tags = got[pl.ds(size.pieces - 1, N, stride=size.pieces), :]
    across = tags.T[0:16, :].astype(i32)
    failed = jnp.max(across[size.slots : size.slots + 1], axis=1, keepdims=True)
    across = across[0 : size.slots]
    lane = iota((N, 128), 1)
    for r in range(size.slots):
        rows = pl.ds(r * N, N)
        t0, t1, t2, t3 = widen(*(got[pl.ds(3 * r + j, N, stride=size.pieces), :] for j in range(3)))
        t0 = jnp.where(lane == TAG, pltpu.roll(tags, TAG - r, 1), t0)
        for j, t in enumerate((t0, t1, t2, t3)):
            h, l = split(t)
            high[rows, j * 128 : (j + 1) * 128] = h
            low[rows, j * 128 : (j + 1) * 128] = l
    kinds = -(-(size.group + 1) // 8) * 8
    height = size.slots * kinds
    spread = [jnp.broadcast_to(across[r : r + 1], (kinds, N)) for r in range(size.slots)]
    spread = jnp.concatenate(spread, axis=0)
    kind = iota((height, N), 0) % kinds
    flags = (spread > 0) & (shift(spread, 11) == kind)
    ones_at = onehot(flags)
    before = onehot(iota((N, N), 0) < iota((N, N), 1))
    count = dot(ones_at, before)
    total = dot(ones_at, jnp.ones((N, N), bf16))
    rows, columns = iota((height, height), 0), iota((height, height), 1)
    earlier = onehot((rows % kinds == columns % kinds) & (columns < rows))
    count = count + dot(earlier, total.astype(bf16))
    member = count < jnp.where(kind == 0, LIST, size.forward).astype(f32)
    failed = jnp.maximum(failed, jnp.max(jnp.where(flags & ~member, 1.0, 0.0)).astype(i32))
    first = jnp.where(kind == 0, 0, LIST + (kind - 1) * size.forward)
    place = jnp.where(flags & member, count + first.astype(f32), -1.0)
    order = iota((LIST + size.relay, 128), 0)
    for r in range(size.slots):
        here = jnp.max(place[r * kinds : (r + 1) * kinds], axis=0, keepdims=True).astype(i32)
        ones[:, r * N : (r + 1) * N] = onehot(order == here)
    lost[...] = failed
    out = dot(ones[...], high[...]) + dot(ones[...], low[...])
    mine[...] = out[0:LIST]
    out = out[LIST:]
    called = CALL * (iota((size.relay, WIDE), 0) // size.forward + 1).astype(f32)
    mark = (iota((size.relay, WIDE), 1) == TAG) & (out > 0.0)
    relay[...] = out - jnp.where(mark, called, 0.0)


def clear(message, scale):
    return jnp.where((iota(message.shape, 1) & 127) < M, message * scale, 0.0)


def place_kernel(unroll, scale, pig, mine, base, out, total, dense, arrive, leave):
    fetch = parts(base, total, arrive)
    for copy in fetch:
        copy.start()
    rows = pigment_rows(pig)
    rowsb = rows.astype(bf16)
    rowst = jnp.concatenate([rows[0:K, 0:128], jnp.zeros((128 - K, 128), f32)], axis=0).T
    rowst = rowst[0:M, 0:K].astype(bf16)
    message = mine[...]
    tag = message[:, 0:128].T[TAG : TAG + 1, :].astype(i32)
    placed = pick(onehot(iota((Q, LIST), 0) + 1 == tag), clear(message, scale))
    for j in range(4):
        dense[j] = tile(placed, j)
    blank = jnp.zeros((128 - 2 * K, 128), f32)
    give = parts(total, out, leave)

    def one(a):
        here = items(a)
        row = jnp.concatenate([dense[0, here, :], dense[1, here, :]], axis=1)
        high, low = split(row)
        new = dot(rowst, high) + dot(rowst, low)
        column = jnp.concatenate([dense[2, here, :], dense[3, here, :], blank], axis=0).T
        high, low = split(column[0:M, 0 : 2 * K])
        new = new + dot(high, rowsb) + dot(low, rowsb)
        store_aux(total, a, aux(total, a) + new)

    for j in range(A // PART):
        fetch[j].wait()
        each(j * PART, (j + 1) * PART, unroll, one)
        give[j].start()
    for copy in give:
        copy.wait()


def few(size, pig, scale, relay):
    message = relay[...]
    head = message[:, 0:128]
    if size.relay < 128:
        head = jnp.concatenate([head, jnp.zeros((128 - size.relay, 128), f32)], axis=0)
    tag = head.T[TAG : TAG + 1, 0 : size.relay]
    flag = jnp.where(tag > 0.5, 1.0, 0.0)
    before = onehot(iota((size.relay, size.relay), 0) < iota((size.relay, size.relay), 1))
    place = dot(jnp.broadcast_to(flag, (8, size.relay)).astype(bf16), before)[0:1, :]
    place = jnp.where(tag > 0.5, place, -1.0).astype(i32)
    message = pick(onehot(iota((size.few, size.relay), 0) == place), message)
    tag = message[:, TAG : TAG + 1].astype(i32)
    message = clear(message, scale)
    who = shift((tag - 1) * 1639, 16)
    who = jnp.where(tag > 0, who, -1)
    mode = tag - 1 - who * K
    lane = iota((size.few, 128), 1)
    at = jnp.sum(jnp.where(lane == mode, pigment_lanes(pig), 0).astype(f32), axis=1, keepdims=True)
    at = at.astype(i32)
    ones = jnp.where(lane == at, 1.0, 0.0)
    zero = jnp.zeros((size.few, 128), f32)
    high = message.astype(bf16).astype(f32)
    low = message - high
    rest = size.factor - 6 * size.few
    left = [ones, ones, tile(high, 2), tile(low, 2), tile(high, 3), tile(low, 3), jnp.zeros((rest, 128), f32)]
    left = jnp.concatenate(left, axis=0)
    owner = jnp.concatenate([who.astype(f32)] * 6 + [jnp.full((rest, 1), -1.0, f32)], axis=0)
    left = jnp.where(iota((size.factor, 128), 1) == M, owner, left).T
    real = jnp.concatenate([ones, zero], axis=1)
    imaginary = jnp.concatenate([zero, ones], axis=1)
    right = [high[:, 0:256], low[:, 0:256], real, real, imaginary, imaginary, jnp.zeros((rest, 256), f32)]
    right = jnp.concatenate(right, axis=0)
    return left[0:M], left[M : M + 1].astype(i32), right.astype(bf16)


def add_few(ref, j, left, whom, right):
    span = range(j * PART, (j + 1) * PART)
    factors = jnp.concatenate([jnp.where(whom == a, left, 0.0).astype(bf16) for a in span], axis=0)
    new = dot(factors, right)
    for n, a in enumerate(span):
        store_aux(ref, a, aux(ref, a) + new[n * M : (n + 1) * M])


def middle_kernel(
    size, pig, relay, partial, listed, slots, lost, out, send, middle, table, chosen, arrive, leave, other
):
    fetch = parts(partial, middle, arrive)
    for copy in fetch:
        copy.start()
    choose = pltpu.make_async_copy(listed, chosen, other)
    choose.start()
    factors = few(size, pig, HALF, relay)
    rows = pigment_rows(pig).astype(bf16)
    give = parts(middle, out, leave)
    for j in range(A // PART):
        fetch[j].wait()
        add_few(middle, j, *factors)
        give[j].start()
        each(j * PART, (j + 1) * PART, size.unroll, lambda a: table_aux(aux(middle, a), rows, a, table))
    choose.wait()
    fill(size, table, chosen, slots, jnp.maximum(slots[4:5, 0:1], lost[...].astype(f32)), send)
    for copy in give:
        copy.wait()


def close_kernel(size, pig, relay, partial, out, total, matrix, arrive, leave):
    fetch = parts(partial, total, arrive)
    for copy in fetch:
        copy.start()
    factors = few(size, pig, STEP, relay)
    give = []
    for j in range(A // PART):
        fetch[j].wait()
        add_few(total, j, *factors)
        span = pl.ds(j * PART, PART)

        def fold(m):
            pieces = []
            for i in range(2):
                for h in range(2):
                    pieces.append(total[h, pl.ds(j * PART * ROWS + 2 * m + i, PART, stride=ROWS), :])
            for i, piece in enumerate(narrow(*pieces)):
                matrix[span, lanes(m * 384 + i * 128)] = piece

        each(0, M // 2, size.unroll * 6, fold)
        give.append(pltpu.make_async_copy(matrix.at[span, :], out.at[span, :], leave.at[j]))
        give[j].start()
    for copy in give:
        copy.wait()


def call(kernel, in_specs, outs, scratch, out_specs):
    return pl.pallas_call(
        kernel,
        in_specs=in_specs,
        out_specs=out_specs,
        out_shape=[jax.ShapeDtypeStruct(*o) for o in outs],
        scratch_shapes=[s if not isinstance(s, tuple) else pltpu.VMEM(*s) for s in scratch],
        compiler_params=pltpu.CompilerParams(vmem_limit_bytes=60 * 1024 * 1024),
    )


def on_device(
    density,
    up_link,
    down_link,
    occupation,
    pigments,
    hamiltonian,
    dipole,
    damping_rates,
    coupling_re,
    coupling_im,
    field,
    pulse_steps,
):
    big = ((2, A * ROWS, 128), f32)
    listing = ((LIST, Q), bf16)
    dense = ((4, Q, 128), f32)
    sems = pltpu.SemaphoreType.DMA((A // PART,))
    pig = pigments.reshape(1, K)

    def begin(size):
        return call(
            functools.partial(open_kernel, size),
            [VMEM] * 6 + [HBM],
            [big, ((N * size.pieces, 128), f32), listing, ((8, LIST), f32)],
            [
                big,
                listing,
                ((A, 2 * M * M), f32),
                dense,
                ((128, 128), f32),
                sems,
                pltpu.SemaphoreType.DMA((2,)),
            ],
            [HBM, VMEM, HBM, VMEM],
        )(
            pig,
            coupling_re.reshape(1, K),
            coupling_im.reshape(1, K),
            up_link,
            down_link,
            occupation,
            density,
        )

    def step(size, section, scale, state, x, send):
        got = lax.all_to_all(
            send.reshape(N, 1, size.pieces * 128), "ha", split_axis=0, concat_axis=0, tiled=True
        )
        base = call(
            functools.partial(commutator_kernel, min(size.unroll, 1), section, scale),
            [SMEM, SMEM] + [VMEM] * 4 + [HBM] * 2,
            [big],
            [big, big, big, ((256, 256), f32), ((A, 128), f32), sems, sems, sems],
            [HBM],
        )(field, pulse_steps, damping_rates.reshape(1, K), occupation, hamiltonian, dipole, state, x)[0]
        got, base = lax.optimization_barrier((got, base))
        ahead = ((size.slots * N, WIDE), bf16)
        mine, relay, lost = call(
            functools.partial(receive_kernel, size),
            [VMEM],
            [((LIST, WIDE), f32), ((size.relay, WIDE), f32), ((1, 1), i32)],
            [ahead, ahead, ((LIST + size.relay, size.slots * N), bf16)],
            [VMEM, VMEM, VMEM],
        )(got.reshape(N * size.pieces, 128))
        relay = lax.all_to_all(
            relay.reshape(size.group, size.forward, WIDE),
            "ha",
            split_axis=0,
            concat_axis=0,
            tiled=True,
            axis_index_groups=[[i + j for j in range(size.group)] for i in range(0, N, size.group)],
        ).reshape(size.relay, WIDE)
        partial = call(
            functools.partial(place_kernel, min(size.unroll, 8), scale),
            [VMEM, VMEM, HBM],
            [big],
            [big, dense, sems, sems],
            [HBM],
        )(pig, mine, base)[0]
        return relay, partial, lost

    def finish(size, state, relay, partial, lost, listed, slots):
        middle, send = call(
            functools.partial(middle_kernel, size),
            [VMEM, VMEM, HBM, HBM, VMEM, VMEM],
            [big, ((N * size.pieces, 128), f32)],
            [big, dense, listing, sems, sems, pltpu.SemaphoreType.DMA],
            [HBM, VMEM],
        )(pig, relay, partial, listed, slots, lost)
        relay, partial, lost = step(size, 1, STEP, state, middle, send)
        return call(
            functools.partial(close_kernel, size),
            [VMEM, VMEM, HBM],
            [((A, 2 * M * M), f32)],
            [big, ((A, 2 * M * M), f32), sems, sems],
            [HBM],
        )(pig, relay, partial)[0], lost.reshape(())

    state, send, listed, slots = begin(MOST)
    relay, partial, lost = step(MOST, 0, HALF, state, state, send)

    def again():
        state, send, listed, slots = begin(EVERY)
        relay, partial, lost = step(EVERY, 0, HALF, state, state, send)
        return finish(EVERY, state, relay, partial, lost, listed, slots)[0]

    out, lost = finish(MOST, state, relay, partial, lost, listed, slots)

    return lax.cond(lost > 0, again, lambda: out)


def solution(mesh):
    rows = P("ha", None)
    return jax.shard_map(
        on_device,
        mesh=mesh,
        in_specs=(rows, rows, rows, rows) + (P(),) * 8,
        out_specs=rows,
        check_vma=False,
    )
```
